32 devices in a mesh: seq: 8 (over z, y), ch: 4 (over x, core).
Axes of the slice: x: 2, y: 2, z: 4, core: 2. Of those that a mesh axis runs over, the one named last changes fastest.
Arguments:
- genome: int32 [2048, 128], P('seq'), may hold values from 0 to 3
- stem_weight: bfloat16 [768, 512], P('ch'), may hold values from -0.5 to 0.5
- dilated_filter_weight: bfloat16 [5, 3, 768, 768], P(None, None, 'ch'), may hold values from -0.125 to 0.125
- head_weight: bfloat16 [768, 5313], P('ch'), may hold values from -0.21875 to 0.21875
- window_start: int32 [128], replicated, may hold values from 0 to 2032
- window_track: int32 [128], replicated, may hold values from 0 to 5312
- targets: float32 [128], replicated, may hold values from 0 to 3
Outputs:
- window_score: float32 [128], replicated
- conv_grad: float32 [5, 3, 768, 768], P(None, None, 'ch', 'seq')
- stem_grad: float32 [768, 512], P('ch')
- head_grad: float32 [768, 5313], P('ch')
The draws below stay inside these ranges and needn't reach their ends.
Inputs may be any that keep to these rules, and one draw needn't show every extreme that they name: `window_start`: each window lies inside the sequence.
All inputs are finite; a program needn't handle non-finite values.
Results may differ from the reference program's by a relative error of at most 0.0037.
Values may be sent and summed in bfloat16 or wider, within the bound.
No kernel may reach another device: no remote copies, remote signals or barrier semaphores. Data moves between devices by JAX's collectives and lax.ppermute only.
A program may use at most 128 MiB of HBM per device.

```python
import math
import jax
import jax.numpy as jnp
import numpy as np
from jax import lax

C = 768
TRACKS = 5313
POOL = 128
ROWS = 256
LAYERS = 5
WIN = 16
BINS = 2048
WINDOWS = 128


def touch_ends(values, own_key, low, top_value):
    spot = [jax.random.randint(jax.random.fold_in(own_key, axis), (), 0, length) for axis, length in enumerate(values.shape)]
    main_axis = values.shape.index(max(values.shape))
    next_to = spot[:main_axis] + [(spot[main_axis] + 1) % values.shape[main_axis]] + spot[main_axis + 1:]
    return values.at[tuple(spot)].set(low).at[tuple(next_to)].set(top_value)


def shard_levels(own_key, extent, cuts, smallest, top_value):
    level = 1.0
    for axis_at, shards_of in cuts:
        heights = jax.random.uniform(jax.random.fold_in(jax.random.fold_in(own_key, 6), axis_at), (shards_of,), jnp.float32, smallest / len(cuts), top_value / len(cuts))
        level = level * jnp.repeat(jnp.exp(heights), extent[axis_at] // shards_of).reshape((-1,) + (1,) * (len(extent) - 1 - axis_at))
    return level


def rank_bounds(number_of, skew):
    portions = [(1 << 20) // math.isqrt(grade ** skew) + 1 for grade in range(1, number_of + 1)]
    deviation = 1 + sum(portions) // (1 << 30)
    return np.cumsum(np.array([max(1, weight // deviation) for weight in portions]))


def ranked(rng, extent, count, skew):
    listing = rank_bounds(count, skew)
    ticket = jax.random.randint(jax.random.fold_in(rng, 1), extent, 0, int(listing[count - 1]))
    standing = jnp.searchsorted(jnp.asarray(listing, jnp.int32), ticket, side="right")
    return jax.random.permutation(jax.random.fold_in(rng, 2), count)[standing].astype(jnp.int32)


def gaussian(key, extent, width, most, shards=(), kind=jnp.bfloat16):
    array = width * jax.random.normal(key, extent, jnp.float32)
    if shards:
        array = array * shard_levels(key, extent, shards, -0.22, 0.18)
    return jnp.clip(array, -most, most).astype(kind)


def setup_inputs(seed: int = 0) -> dict:
    keys = jax.random.split(jax.random.key(seed), 8)
    genome = touch_ends(jax.random.randint(keys[0], (BINS, POOL), 0, 4), jax.random.fold_in(keys[0], 1), 0, 3).astype(jnp.int32)
    stem_weight = gaussian(keys[1], (C, 4 * POOL), POOL ** -0.5, 0.5, ((0, 4),))
    dilated_filter_weight = gaussian(keys[2], (LAYERS, 3, C, C), (3 * C) ** -0.5, 0.125, ((2, 4),))
    head_weight = gaussian(keys[3], (C, TRACKS), C ** -0.5, 0.21875, ((0, 4),))
    window_start = touch_ends(jax.random.randint(keys[4], (WINDOWS,), 0, BINS - WIN + 1), jax.random.fold_in(keys[4], 1), 0, BINS - WIN).astype(jnp.int32)
    window_track = touch_ends(ranked(keys[5], (WINDOWS,), TRACKS, 2), jax.random.fold_in(keys[5], 3), 0, TRACKS - 1).astype(jnp.int32)
    targets = jnp.clip(jax.random.uniform(keys[6], (WINDOWS,), jnp.float32, 0.0, 3.0), 0.0, 3.0)
    return dict(genome=genome, stem_weight=stem_weight, dilated_filter_weight=dilated_filter_weight, head_weight=head_weight, window_start=window_start, window_track=window_track, targets=targets)


def dilations(shard_rows):
    return (shard_rows // 8, shard_rows // 2, shard_rows, 2 * shard_rows, 4 * shard_rows)

def moved(field, offset):
    length = field.shape[-1]
    blanks = jnp.zeros(field.shape[:-1] + (abs(offset),), field.dtype)
    if offset > 0:
        return jnp.concatenate([field[..., offset:], blanks], axis=-1)
    return jnp.concatenate([blanks, field[..., :length + offset]], axis=-1)

def order_taps(lower_rows, middle, upper_rows):
    forward_taps = jnp.stack([lower_rows[0], middle[0], upper_rows[0]])
    reverse_taps = jnp.stack([upper_rows[1], middle[1], lower_rows[1]])
    return jnp.stack([forward_taps, reverse_taps])

def reference(genome, stem_weight, dilated_filter_weight, head_weight, window_start, window_track, targets):
    spans = dilations(ROWS)
    letters = (genome[:, :, None] == jnp.arange(4, dtype=jnp.int32)).astype(jnp.bfloat16).reshape(BINS, 4 * POOL)
    strands = jnp.stack([letters, letters[:, ::-1]])
    residual_state = jnp.einsum('sri,ci->scr', strands.astype(jnp.float32), stem_weight.astype(jnp.float32))
    saved_states = []
    stored_taps = []
    for current_layer_index in range(LAYERS):
        active = jax.nn.gelu(residual_state).astype(jnp.bfloat16)
        reach_now = spans[current_layer_index]
        resident_taps = order_taps(moved(active, -reach_now), active, moved(active, reach_now))
        saved_states.append(residual_state)
        stored_taps.append(resident_taps)
        residual_state = residual_state + jnp.einsum('nezp,efz->nfp', resident_taps.astype(jnp.float32), dilated_filter_weight[current_layer_index].astype(jnp.float32))
    strand_total = residual_state[0] + residual_state[1]
    positions = jnp.arange(BINS, dtype=jnp.int32)
    member = ((positions[None, :] >= window_start[:, None]) & (positions[None, :] < window_start[:, None] + WIN)).astype(jnp.float32)
    pooled = jnp.einsum('cr,kr->ck', strand_total, member, precision=lax.Precision.HIGHEST) / WIN
    columns = jnp.take(head_weight, window_track, axis=1).astype(jnp.float32)
    window_score = 0.5 * lax.optimization_barrier(jnp.sum(pooled * columns, axis=0))
    counts = lax.optimization_barrier(jnp.sum((window_track[:, None] == window_track[None, :]).astype(jnp.float32), axis=1))
    loss_slope = (jnp.exp(window_score) - targets) / counts
    head_grad = jnp.zeros(head_weight.shape, jnp.float32).at[:, window_track].add(0.5 * loss_slope[None, :] * pooled)
    weights_back = 0.5 / WIN * loss_slope[None, :] * columns
    back_total = jnp.einsum('ck,kr->cr', weights_back, member, precision=lax.Precision.HIGHEST)
    grad_state = jnp.stack([back_total, back_total])
    layer_gradient_list = []
    for current_layer_index in reversed(range(LAYERS)):
        incoming_gradient = grad_state.astype(jnp.bfloat16)
        layer_gradient_list.append(jnp.einsum('pygj,pij->yig', stored_taps[current_layer_index].astype(jnp.float32), incoming_gradient.astype(jnp.float32)))
        reach_now = spans[current_layer_index]
        back_taps = order_taps(moved(incoming_gradient, reach_now), incoming_gradient, moved(incoming_gradient, -reach_now))
        spread = jnp.einsum('skor,koc->scr', back_taps.astype(jnp.float32), dilated_filter_weight[current_layer_index].astype(jnp.float32))
        pullback = jax.vjp(jax.nn.gelu, saved_states[current_layer_index])[1]
        grad_state = grad_state + pullback(spread)[0]
    conv_grad = jnp.stack(layer_gradient_list[::-1])
    stem_grad = jnp.einsum('sri,scr->ci', strands.astype(jnp.float32), grad_state.astype(jnp.bfloat16).astype(jnp.float32))
    return (window_score, conv_grad, stem_grad, head_grad)
```

```python
import jax
import jax.numpy as jnp
from jax import lax
from jax.sharding import PartitionSpec as P

LAYERS = 5
WIN = 16
CORES = 2

bf16 = jnp.bfloat16
f32 = jnp.float32


def dilations(shard_rows):
    return (shard_rows // 8, shard_rows // 2, shard_rows, 2 * shard_rows, 4 * shard_rows)


def core_swap(value):
    count = lax.axis_size("ch")
    return lax.ppermute(value, "ch", [(i, i ^ 1) for i in range(count)])


def chip_shift(value, by):
    count = lax.axis_size("ch")
    return lax.ppermute(value, "ch", [(i, (i + CORES * by) % count) for i in range(count)])


def seq_swap(value, bit):
    count = lax.axis_size("seq")
    return lax.ppermute(value, "seq", [(i, i ^ bit) for i in range(count)])


def choose(index, options):
    picked = options[0]
    for place, option in enumerate(options[1:], 1):
        picked = jnp.where(index == place, option, picked)
    return picked


def rolled(field, by):
    if by == 0:
        return field
    blank = jnp.zeros((abs(by),) + field.shape[1:], field.dtype)
    if by > 0:
        return jnp.concatenate([field[by:], blank], axis=0)
    return jnp.concatenate([blank, field[:by]], axis=0)


def chip_gather(own, chip, chips):
    parts = [own] + [chip_shift(own, by) for by in range(1, chips)]
    return jnp.concatenate(
        [choose((chip - place) % chips, parts) for place in range(chips)], axis=1
    )


def chip_scatter(total, chip, chips):
    parts = jnp.split(total, chips, axis=1)
    mine = choose(chip, parts)
    for by in range(1, chips):
        mine = mine + chip_shift(choose((chip + by) % chips, parts).astype(bf16), by).astype(f32)
    return mine


def seq_scatter(total, seq):
    count = lax.axis_size("seq")
    field = total.reshape((count, total.shape[0] // count) + total.shape[1:])
    bit = 1
    while bit < count:
        pairs = field.reshape((field.shape[0] // 2, 2) + field.shape[1:])
        side = (seq // bit) % 2
        mine = choose(side, [pairs[:, 0], pairs[:, 1]])
        other = choose(side, [pairs[:, 1], pairs[:, 0]]).astype(bf16)
        field = mine + seq_swap(other, bit).astype(f32)
        bit *= 2
    return field[0]


def shards(
    genome, stem_weight, dilated_filter_weight, head_weight, window_start, window_track, targets
):
    shard_rows, pool = genome.shape
    seqs = lax.axis_size("seq")
    chips = lax.axis_size("ch") // CORES
    seq = lax.axis_index("seq")
    strand = lax.axis_index("ch") % CORES
    chip = lax.axis_index("ch") // CORES
    spans = dilations(shard_rows)
    classes = spans[0]
    own_classes = classes // seqs
    steps = shard_rows // classes
    reach = tuple(span // classes * own_classes for span in spans)
    quarter = stem_weight.shape[0]

    sibling_stem = core_swap(stem_weight)
    stem_half = jnp.concatenate(
        [choose(strand, [stem_weight, sibling_stem]), choose(strand, [sibling_stem, stem_weight])]
    )
    stem_parts = [stem_half] + [chip_shift(stem_half, by) for by in range(1, chips)]
    stem_full = jnp.concatenate([choose((chip - p) % chips, stem_parts) for p in range(chips)])

    filters = []
    for layer in range(LAYERS):
        own_filter = dilated_filter_weight[layer]
        sibling_filter = core_swap(own_filter)
        filters.append(
            jnp.concatenate(
                [
                    choose(strand, [own_filter, sibling_filter]),
                    choose(strand, [sibling_filter, own_filter]),
                ],
                axis=1,
            )
        )

    blocks = (
        genome.astype(bf16)
        .reshape(steps, seqs, own_classes, pool)
        .transpose(1, 0, 2, 3)
        .reshape(seqs, steps * own_classes, pool)
    )
    blocks = lax.all_to_all(blocks, "seq", 0, 0, tiled=True)
    bases = blocks.reshape(shard_rows, pool)
    row = jnp.arange(shard_rows, dtype=jnp.int32)
    step_of = row // own_classes
    step_of = jnp.where(strand == 0, step_of, shard_rows // own_classes - 1 - step_of)
    class_of = row % own_classes
    source_row = step_of * own_classes + class_of
    order = (source_row[:, None] == row[None, :]).astype(bf16)
    letter = jnp.arange(4 * pool, dtype=jnp.int32)
    place = jnp.where(strand == 0, letter // 4, pool - 1 - letter // 4)
    spread_place = (jnp.arange(pool, dtype=jnp.int32)[:, None] == place[None, :]).astype(bf16)
    base_of = jnp.where(strand == 0, letter % 4, 3 - letter % 4)
    ordered = jnp.dot(order, bases, preferred_element_type=f32).astype(bf16)
    wide = jnp.dot(ordered, spread_place, preferred_element_type=f32)
    letters = (wide == base_of[None, :].astype(f32)).astype(bf16)
    position = step_of * classes + seq * own_classes + class_of

    member = (
        (position[None, :] >= window_start[:, None])
        & (position[None, :] < window_start[:, None] + WIN)
    ).astype(f32)
    columns = jnp.take(head_weight, window_track, axis=1)
    sibling_columns = core_swap(columns)
    half_columns = jnp.concatenate(
        [choose(strand, [columns, sibling_columns]), choose(strand, [sibling_columns, columns])]
    ).astype(f32)
    counts = jnp.sum((window_track[:, None] == window_track[None, :]).astype(f32), axis=1)

    whole = lax.dot_general(
        letters, stem_full, (((1,), (1,)), ((), ())), preferred_element_type=f32
    )
    active = jax.nn.gelu(whole).astype(bf16)
    stream = choose(chip, jnp.split(whole, chips, axis=1))
    streams = []
    actives = []
    for layer in range(LAYERS):
        streams.append(stream)
        actives.append(active)
        for tap in range(3):
            stream = stream + lax.dot_general(
                rolled(active, (tap - 1) * reach[layer]),
                filters[layer][tap],
                (((1,), (1,)), ((), ())),
                preferred_element_type=f32,
            )
        if layer < LAYERS - 1:
            active = chip_gather(jax.nn.gelu(stream).astype(bf16), chip, chips)

    pooled = (
        lax.dot_general(
            stream, member, (((0,), (1,)), ((), ())), precision=lax.Precision.HIGHEST
        )
        / WIN
    )
    partial_score = 0.5 * jnp.sum(pooled * half_columns, axis=0)
    everyone = seqs * chips * CORES
    scores = lax.all_to_all(
        jnp.broadcast_to(partial_score, (everyone,) + partial_score.shape),
        ("seq", "ch"),
        0,
        0,
        tiled=True,
    )
    window_score = jnp.sum(scores, axis=0)
    loss_slope = (jnp.exp(window_score) - targets) / counts

    pooled_parts = [pooled[:quarter], pooled[quarter:]]
    pooled_own = choose(strand, pooled_parts) + core_swap(choose(1 - strand, pooled_parts))
    bit = 1
    while bit < seqs:
        pooled_own = pooled_own + seq_swap(pooled_own, bit)
        bit *= 2
    head_grad = (
        jnp.zeros(head_weight.shape, f32)
        .at[:, window_track]
        .add(0.5 * loss_slope[None, :] * pooled_own)
    )

    weights_back = 0.5 / WIN * loss_slope[None, :] * half_columns
    grad = lax.dot_general(
        member, weights_back, (((0,), (1,)), ((), ())), precision=lax.Precision.HIGHEST
    )
    filter_grads = []
    for layer in reversed(range(LAYERS)):
        upstream = grad.astype(bf16)
        taps = [rolled(upstream, (1 - tap) * reach[layer]) for tap in range(3)]
        back = sum(
            jnp.dot(taps[tap], filters[layer][tap], preferred_element_type=f32)
            for tap in range(3)
        )
        halves = [
            jnp.concatenate([tap[:, :quarter] for tap in taps], axis=1),
            jnp.concatenate([tap[:, quarter:] for tap in taps], axis=1),
        ]

        def filter_part(half):
            return lax.dot_general(
                actives[layer], half, (((0,), (0,)), ((), ())), preferred_element_type=f32
            )

        theirs = filter_part(choose(1 - strand, halves)).astype(bf16)
        ours = filter_part(choose(strand, halves)) + core_swap(theirs).astype(f32)
        filter_grads.append(seq_scatter(ours, seq))
        through = chip_scatter(back, chip, chips)
        pullback = jax.vjp(jax.nn.gelu, streams[layer])[1]
        grad = grad + pullback(through)[0]

    conv_grad = jnp.stack(
        [g.reshape(g.shape[0], 3, quarter).transpose(1, 2, 0) for g in filter_grads[::-1]]
    )

    stem_part = lax.dot_general(
        grad.astype(bf16), letters, (((0,), (0,)), ((), ())), preferred_element_type=f32
    )
    stem_parts = [stem_part[:quarter], stem_part[quarter:]]
    stem_own = choose(strand, stem_parts) + core_swap(
        choose(1 - strand, stem_parts).astype(bf16)
    ).astype(f32)
    blocks = lax.all_to_all(
        stem_own.astype(bf16).reshape(seqs, quarter // seqs, -1), "seq", 0, 0, tiled=True
    )
    stem_block = jnp.sum(blocks.astype(f32), axis=0)
    stem_grad = lax.all_to_all(
        jnp.broadcast_to(stem_block, (seqs,) + stem_block.shape), "seq", 0, 0, tiled=True
    ).reshape(quarter, -1)
    return (window_score, conv_grad, stem_grad, head_grad)


def solution(mesh):
    return jax.shard_map(
        shards,
        mesh=mesh,
        in_specs=(
            P("seq", None),
            P("ch", None),
            P(None, None, "ch", None),
            P("ch", None),
            P(),
            P(),
            P(),
        ),
        out_specs=(P(), P(None, None, "ch", "seq"), P("ch", None), P("ch", None)),
        check_vma=False,
    )
```

```python
import jax
import jax.numpy as jnp
from jax import lax
from jax.sharding import PartitionSpec as P

LAYERS = 5
WIN = 16
CORES = 2

bf16 = jnp.bfloat16
f32 = jnp.float32


def dilations(shard_rows):
    return (shard_rows // 8, shard_rows // 2, shard_rows, 2 * shard_rows, 4 * shard_rows)


def core_swap(value):
    count = lax.axis_size("ch")
    return lax.ppermute(value, "ch", [(i, i ^ 1) for i in range(count)])


def chip_shift(value, by):
    count = lax.axis_size("ch")
    return lax.ppermute(value, "ch", [(i, (i + CORES * by) % count) for i in range(count)])


def seq_swap(value, bit):
    count = lax.axis_size("seq")
    return lax.ppermute(value, "seq", [(i, i ^ bit) for i in range(count)])


def choose(index, options):
    picked = options[0]
    for place, option in enumerate(options[1:], 1):
        picked = jnp.where(index == place, option, picked)
    return picked


def rolled(field, by):
    if by == 0:
        return field
    blank = jnp.zeros((abs(by),) + field.shape[1:], field.dtype)
    if by > 0:
        return jnp.concatenate([field[by:], blank], axis=0)
    return jnp.concatenate([blank, field[:by]], axis=0)


def chip_scatter_parts(total, chip, chips):
    parts = jnp.split(total, chips, axis=1)
    sends = [choose((chip + by) % chips, parts).astype(bf16) for by in range(1, chips)]
    return choose(chip, parts), sends


def tied(*values):
    return lax.optimization_barrier(values)


def by_strand(strand, own, sibling):
    return [jnp.where(strand == 0, own, sibling), jnp.where(strand == 0, sibling, own)]


def pieces(value):
    high = value.astype(bf16)
    rest = value - high.astype(f32)
    middle = rest.astype(bf16)
    return high, middle, (rest - middle.astype(f32)).astype(bf16)


class BlockSum:
    def __init__(self, kept, sent):
        self.kept, self.sent = kept, sent
        self.bit = 1

    def move(self):
        return seq_swap(self.sent, self.bit)

    def join(self, received):
        total = self.kept + received.astype(f32)
        half = total.shape[0] // 2
        self.bit *= 2
        if self.bit < lax.axis_size("seq"):
            self.kept, self.sent = total[:half], total[half:].astype(bf16)
        else:
            self.kept, self.sent = total, None


def shards(
    genome, stem_weight, dilated_filter_weight, head_weight, window_start, window_track, targets
):
    shard_rows, pool = genome.shape
    seqs = lax.axis_size("seq")
    chips = lax.axis_size("ch") // CORES
    seq = lax.axis_index("seq")
    strand = lax.axis_index("ch") % CORES
    chip = lax.axis_index("ch") // CORES
    spans = dilations(shard_rows)
    classes = spans[0]
    own_classes = classes // seqs
    steps = shard_rows // classes
    reach = tuple(span // classes * own_classes for span in spans)
    quarter = stem_weight.shape[0]
    channels = dilated_filter_weight.shape[3]
    block = channels // seqs
    tracks = head_weight.shape[1]

    blocks = (
        genome.astype(bf16)
        .reshape(steps, seqs, own_classes, pool)
        .transpose(1, 0, 2, 3)
        .reshape(seqs, steps * own_classes, pool)
    )
    blocks = lax.all_to_all(blocks, "seq", 0, 0, tiled=True)

    stem_own = [stem_weight] + [chip_shift(stem_weight, by) for by in range(1, chips)]
    stem_pairs = [
        jnp.concatenate(by_strand(strand, part, core_swap(part))) for part in stem_own
    ]
    stem_full = jnp.concatenate([choose((chip - p) % chips, stem_pairs) for p in range(chips)])

    sibling_filter = core_swap(dilated_filter_weight)

    def filter_of(layer):
        return jnp.concatenate(
            by_strand(strand, dilated_filter_weight[layer], sibling_filter[layer]), axis=1
        )

    bases = blocks.reshape(shard_rows, pool)
    row = jnp.arange(shard_rows, dtype=jnp.int32)
    step_of = row // own_classes
    step_of = jnp.where(strand == 0, step_of, shard_rows // own_classes - 1 - step_of)
    class_of = row % own_classes
    source_row = step_of * own_classes + class_of
    order = (source_row[:, None] == row[None, :]).astype(bf16)
    letter = jnp.arange(4 * pool, dtype=jnp.int32)
    place = jnp.where(strand == 0, letter // 4, pool - 1 - letter // 4)
    spread_place = (jnp.arange(pool, dtype=jnp.int32)[:, None] == place[None, :]).astype(bf16)
    base_of = jnp.where(strand == 0, letter % 4, 3 - letter % 4)
    ordered = jnp.dot(order, bases, preferred_element_type=f32).astype(bf16)
    wide = jnp.dot(ordered, spread_place, preferred_element_type=f32)
    letters = (wide == base_of[None, :].astype(f32)).astype(bf16)
    position = step_of * classes + seq * own_classes + class_of

    member = (
        (position[None, :] >= window_start[:, None])
        & (position[None, :] < window_start[:, None] + WIN)
    ).astype(f32)
    counts = jnp.sum((window_track[:, None] == window_track[None, :]).astype(f32), axis=1)
    at_track = (
        jnp.arange(tracks, dtype=jnp.int32)[None, :] == window_track[:, None]
    ).astype(bf16)

    bits = seqs.bit_length() - 1
    slot = jnp.arange(channels, dtype=jnp.int32) // block
    away = sum(((slot >> (bits - 1 - b)) & 1) << b for b in range(bits))
    wanted = (seq ^ away) * block + jnp.arange(channels, dtype=jnp.int32) % block
    by_distance = (
        jnp.arange(channels, dtype=jnp.int32)[:, None] == wanted[None, :]
    ).astype(bf16)

    whole = lax.dot_general(
        letters, stem_full, (((1,), (1,)), ((), ())), preferred_element_type=f32
    )
    active = jax.nn.gelu(whole).astype(bf16)
    stream = choose(chip, jnp.split(whole, chips, axis=1))
    filters = [filter_of(0)]
    streams = []
    actives = []
    for layer in range(LAYERS):
        streams.append(stream)
        for tap in range(3):
            stream = stream + lax.dot_general(
                rolled(active, (tap - 1) * reach[layer]),
                filters[layer][tap],
                (((1,), (1,)), ((), ())),
                preferred_element_type=f32,
            )
        if layer < LAYERS - 1:
            own = jax.nn.gelu(stream).astype(bf16)
            (own,) = tied(own)
            parts = [chip_shift(own, by) for by in range(1, chips)]
            beside = [
                filter_of(layer + 1),
                jnp.dot(active, by_distance, preferred_element_type=f32).astype(bf16),
            ]
            if layer == 0:
                columns = lax.dot_general(
                    head_weight, at_track, (((1,), (1,)), ((), ())), preferred_element_type=f32
                ).astype(bf16)
                beside.append(columns)
            if layer == 1:
                beside.append(
                    jnp.concatenate(by_strand(strand, columns, core_swap(columns))).astype(f32)
                )
            parts, beside = tied(parts, beside)
            filters.append(beside[0])
            actives.append(beside[1])
            if layer == 0:
                columns = beside[2]
            if layer == 1:
                half_columns = beside[2]
            parts = [own] + list(parts)
            active = jnp.concatenate(
                [choose((chip - p) % chips, parts) for p in range(chips)], axis=1
            )

    pooled = (
        lax.dot_general(
            stream, member, (((0,), (1,)), ((), ())), precision=lax.Precision.HIGHEST
        )
        / WIN
    )
    partial_score = 0.5 * jnp.sum(pooled * half_columns, axis=0)
    everyone = seqs * chips * CORES
    scores = lax.all_to_all(
        jnp.broadcast_to(partial_score, (everyone,) + partial_score.shape),
        ("seq", "ch"),
        0,
        0,
        tiled=True,
    )
    pooled_parts = [pooled[:quarter], pooled[quarter:]]
    pooled_own = choose(strand, pooled_parts) + core_swap(choose(1 - strand, pooled_parts))
    last_active = jnp.dot(active, by_distance, preferred_element_type=f32).astype(bf16)
    scores, pooled_own, last_active = tied(scores, pooled_own, last_active)
    actives.append(last_active)
    window_score = jnp.sum(scores, axis=0)
    loss_slope = (jnp.exp(window_score) - targets) / counts

    weights_back = 0.5 / WIN * loss_slope[None, :] * half_columns
    grad = lax.dot_general(
        member, weights_back, (((0,), (1,)), ((), ())), precision=lax.Precision.HIGHEST
    )
    sums = []
    pooled_bit = 1
    for layer in reversed(range(LAYERS)):
        upstream = grad.astype(bf16)
        taps = [rolled(upstream, (1 - tap) * reach[layer]) for tap in range(3)]
        back = sum(
            jnp.dot(taps[tap], filters[layer][tap], preferred_element_type=f32)
            for tap in range(3)
        )
        mine, sends = chip_scatter_parts(back, chip, chips)
        going = [s for s in sums if s.sent is not None]
        sends, seq_sends, taps = tied(sends, [s.sent for s in going], taps)
        for s, sent in zip(going, seq_sends):
            s.sent = sent
        received = [chip_shift(sent, by) for by, sent in enumerate(sends, 1)]
        seq_received = [s.move() for s in going]
        if pooled_bit < seqs:
            pooled_received = seq_swap(pooled_own, pooled_bit)
            pooled_bit *= 2
        else:
            pooled_received = jnp.zeros_like(pooled_own)
        halves = [
            jnp.concatenate([tap[:, :quarter] for tap in taps], axis=1),
            jnp.concatenate([tap[:, quarter:] for tap in taps], axis=1),
        ]
        theirs = lax.dot_general(
            actives[layer],
            choose(1 - strand, halves),
            (((0,), (0,)), ((), ())),
            preferred_element_type=f32,
        ).astype(bf16)
        theirs = core_swap(theirs)
        ours = choose(strand, halves)
        near, far = jnp.split(actives[layer], 2, axis=1)
        keep = lax.dot_general(
            near, ours, (((0,), (0,)), ((), ())), preferred_element_type=f32
        ) + theirs[: channels // 2].astype(f32)
        send = (
            lax.dot_general(far, ours, (((0,), (0,)), ((), ())), preferred_element_type=f32)
            + theirs[channels // 2 :].astype(f32)
        ).astype(bf16)
        received, seq_received, pooled_received, keep, send = tied(
            received, seq_received, pooled_received, keep, send
        )
        for s, got in zip(going, seq_received):
            s.join(got)
        pooled_own = pooled_own + pooled_received
        sums.append(BlockSum(keep, send))
        through = mine
        for got in received:
            through = through + got.astype(f32)
        pullback = jax.vjp(jax.nn.gelu, streams[layer])[1]
        grad = grad + pullback(through)[0]

    stem_part = lax.dot_general(
        grad.astype(bf16), letters, (((0,), (0,)), ((), ())), preferred_element_type=f32
    )
    stem_parts = [stem_part[:quarter], stem_part[quarter:]]
    stem_own = choose(strand, stem_parts) + core_swap(
        choose(1 - strand, stem_parts).astype(bf16)
    ).astype(f32)
    stem_send = stem_own.astype(bf16).reshape(seqs, quarter // seqs, -1)
    going = [s for s in sums if s.sent is not None]
    seq_received = [s.move() for s in going]
    stem_blocks = lax.all_to_all(stem_send, "seq", 0, 0, tiled=True)
    stem_blocks, seq_received, pooled_own = tied(stem_blocks, seq_received, pooled_own)
    for s, got in zip(going, seq_received):
        s.join(got)
    stem_block = jnp.sum(stem_blocks.astype(f32), axis=0)
    stem_grad = lax.all_to_all(
        jnp.broadcast_to(stem_block, (seqs,) + stem_block.shape), "seq", 0, 0, tiled=True
    ).reshape(quarter, -1)
    while pooled_bit < seqs:
        pooled_own = pooled_own + seq_swap(pooled_own, pooled_bit)
        pooled_bit *= 2
    going = [s for s in sums if s.sent is not None]
    while going:
        for s in going:
            s.join(s.move())
        going = [s for s in sums if s.sent is not None]
    head_grad = lax.dot_general(
        jnp.concatenate(pieces(0.5 * loss_slope[None, :] * pooled_own), axis=1),
        jnp.concatenate([at_track] * 3),
        (((1,), (0,)), ((), ())),
        preferred_element_type=f32,
    )
    conv_grad = jnp.stack(
        [s.kept.reshape(block, 3, quarter).transpose(1, 2, 0) for s in sums[::-1]]
    )
    return (window_score, conv_grad, stem_grad, head_grad)


def solution(mesh):
    return jax.shard_map(
        shards,
        mesh=mesh,
        in_specs=(
            P("seq", None),
            P("ch", None),
            P(None, None, "ch", None),
            P("ch", None),
            P(),
            P(),
            P(),
        ),
        out_specs=(P(), P(None, None, "ch", "seq"), P("ch", None), P("ch", None)),
        check_vma=False,
    )
```

```python
import jax
import jax.numpy as jnp
from jax import lax
from jax.experimental import pallas as pl
from jax.experimental.pallas import tpu as pltpu
from jax.sharding import PartitionSpec as P

LAYERS = 5
WIN = 16
CORES = 2

bf16 = jnp.bfloat16
f32 = jnp.float32


def dilations(shard_rows):
    return (shard_rows // 8, shard_rows // 2, shard_rows, 2 * shard_rows, 4 * shard_rows)


def core_swap(value):
    count = lax.axis_size("ch")
    return lax.ppermute(value, "ch", [(i, i ^ 1) for i in range(count)])


def chip_shift(value, by):
    count = lax.axis_size("ch")
    return lax.ppermute(value, "ch", [(i, (i + CORES * by) % count) for i in range(count)])


def seq_swap(value, bit):
    count = lax.axis_size("seq")
    return lax.ppermute(value, "seq", [(i, i ^ bit) for i in range(count)])


def choose(index, options):
    picked = options[0]
    for place, option in enumerate(options[1:], 1):
        picked = jnp.where(index == place, option, picked)
    return picked


def rolled(field, by):
    if by == 0:
        return field
    blank = jnp.zeros((abs(by),) + field.shape[1:], field.dtype)
    if by > 0:
        return jnp.concatenate([field[by:], blank], axis=0)
    return jnp.concatenate([blank, field[:by]], axis=0)


def chip_scatter_parts(total, chip, chips):
    parts = jnp.split(total, chips, axis=1)
    sends = [choose((chip + by) % chips, parts).astype(bf16) for by in range(1, chips)]
    return choose(chip, parts), sends


def tied(*values):
    return lax.optimization_barrier(values)


def by_strand(strand, own, sibling):
    return [jnp.where(strand == 0, own, sibling), jnp.where(strand == 0, sibling, own)]


def pieces(value):
    high = value.astype(bf16)
    rest = value - high.astype(f32)
    middle = rest.astype(bf16)
    return high, middle, (rest - middle.astype(f32)).astype(bf16)


class BlockSum:
    def __init__(self, kept, sent):
        self.kept, self.sent = kept, sent
        self.bit = 1
        self.received = None

    def start(self):
        if self.sent is not None and self.received is None:
            self.received = seq_swap(self.sent, self.bit)

    def join(self):
        self.bit *= 2
        if self.bit < lax.axis_size("seq"):
            total = self.kept + self.received.astype(f32)
            half = total.shape[0] // 2
            self.kept, self.sent = total[:half], total[half:].astype(bf16)
            self.received = None
        else:
            self.sent = None


def assemble(sums, quarter):
    block = sums[0].kept.shape[0]
    taps = sums[0].kept.shape[1] // quarter
    count = len(sums)

    def kernel(*refs):
        out = refs[-1]
        for layer in range(count):
            total = refs[layer][...] + refs[count + layer][...].astype(f32)
            out[layer] = total.T.reshape(taps, quarter, block)

    return pl.pallas_call(
        kernel,
        out_shape=jax.ShapeDtypeStruct((count, taps, quarter, block), f32),
        compiler_params=pltpu.CompilerParams(vmem_limit_bytes=32 << 20),
    )(*[s.kept for s in sums], *[s.received for s in sums])


def shards(
    genome, stem_weight, dilated_filter_weight, head_weight, window_start, window_track, targets
):
    shard_rows, pool = genome.shape
    seqs = lax.axis_size("seq")
    chips = lax.axis_size("ch") // CORES
    seq = lax.axis_index("seq")
    strand = lax.axis_index("ch") % CORES
    chip = lax.axis_index("ch") // CORES
    spans = dilations(shard_rows)
    classes = spans[0]
    own_classes = classes // seqs
    steps = shard_rows // classes
    reach = tuple(span // classes * own_classes for span in spans)
    quarter = stem_weight.shape[0]
    channels = dilated_filter_weight.shape[3]
    block = channels // seqs
    tracks = head_weight.shape[1]

    blocks = (
        genome.astype(bf16)
        .reshape(steps, seqs, own_classes, pool)
        .transpose(1, 0, 2, 3)
        .reshape(seqs, steps * own_classes, pool)
    )
    blocks = lax.all_to_all(blocks, "seq", 0, 0, tiled=True)

    stem_own = [stem_weight] + [chip_shift(stem_weight, by) for by in range(1, chips)]
    stem_pairs = [
        jnp.concatenate(by_strand(strand, part, core_swap(part))) for part in stem_own
    ]
    stem_full = jnp.concatenate([choose((chip - p) % chips, stem_pairs) for p in range(chips)])

    sibling_filter = core_swap(dilated_filter_weight)

    own_filter = dilated_filter_weight

    def filter_of(layer):
        return jnp.concatenate(
            by_strand(strand, own_filter[layer], sibling_filter[layer]), axis=1
        )

    bases = blocks.reshape(shard_rows, pool)
    row = jnp.arange(shard_rows, dtype=jnp.int32)
    step_of = row // own_classes
    step_of = jnp.where(strand == 0, step_of, shard_rows // own_classes - 1 - step_of)
    class_of = row % own_classes
    source_row = step_of * own_classes + class_of
    order = (source_row[:, None] == row[None, :]).astype(bf16)
    letter = jnp.arange(4 * pool, dtype=jnp.int32)
    place = jnp.where(strand == 0, letter // 4, pool - 1 - letter // 4)
    spread_place = (jnp.arange(pool, dtype=jnp.int32)[:, None] == place[None, :]).astype(bf16)
    base_of = jnp.where(strand == 0, letter % 4, 3 - letter % 4)
    ordered = jnp.dot(order, bases, preferred_element_type=f32).astype(bf16)
    wide = jnp.dot(ordered, spread_place, preferred_element_type=f32)
    letters = (wide == base_of[None, :].astype(f32)).astype(bf16)
    position = step_of * classes + seq * own_classes + class_of

    member = (
        (position[None, :] >= window_start[:, None])
        & (position[None, :] < window_start[:, None] + WIN)
    ).astype(bf16)
    counts = jnp.sum((window_track[:, None] == window_track[None, :]).astype(f32), axis=1)
    at_track = (
        jnp.arange(tracks, dtype=jnp.int32)[None, :] == window_track[:, None]
    ).astype(bf16)

    bits = seqs.bit_length() - 1
    slot = jnp.arange(channels, dtype=jnp.int32) // block
    away = sum(((slot >> (bits - 1 - b)) & 1) << b for b in range(bits))
    wanted = (seq ^ away) * block + jnp.arange(channels, dtype=jnp.int32) % block
    by_distance = (
        jnp.arange(channels, dtype=jnp.int32)[:, None] == wanted[None, :]
    ).astype(bf16)

    whole = lax.dot_general(
        letters, stem_full, (((1,), (1,)), ((), ())), preferred_element_type=f32
    )
    active = jax.nn.gelu(whole).astype(bf16)
    stream = choose(chip, jnp.split(whole, chips, axis=1))
    filters = [filter_of(0)]
    streams = []
    actives = []
    for layer in range(LAYERS):
        streams.append(stream)
        for tap in range(3):
            stream = stream + lax.dot_general(
                rolled(active, (tap - 1) * reach[layer]),
                filters[layer][tap],
                (((1,), (1,)), ((), ())),
                preferred_element_type=f32,
            )
        if layer < LAYERS - 1:
            own = jax.nn.gelu(stream).astype(bf16)
            own, own_filter, sibling_filter, by_distance, at_track = tied(
                own, own_filter, sibling_filter, by_distance, at_track
            )
            parts = [chip_shift(own, by) for by in range(1, chips)]
            beside = [
                filter_of(layer + 1),
                jnp.dot(active, by_distance, preferred_element_type=f32).astype(bf16),
            ]
            if layer == 1:
                columns = lax.dot_general(
                    head_weight, at_track, (((1,), (1,)), ((), ())), preferred_element_type=f32
                ).astype(bf16)
                beside.append(columns)
            if layer == 2:
                beside.append(jnp.concatenate(by_strand(strand, columns, core_swap(columns))))
            parts, beside = tied(parts, beside)
            filters.append(beside[0])
            actives.append(beside[1])
            if layer == 1:
                columns = beside[2]
            if layer == 2:
                half_columns = beside[2]
            parts = [own] + list(parts)
            active = jnp.concatenate(
                [choose((chip - p) % chips, parts) for p in range(chips)], axis=1
            )

    pooled = (
        lax.dot_general(
            jnp.concatenate(pieces(stream)),
            jnp.concatenate([member] * 3, axis=1),
            (((0,), (1,)), ((), ())),
            preferred_element_type=f32,
        )
        / WIN
    )
    partial_score = 0.5 * jnp.sum(pooled * half_columns.astype(f32), axis=0)
    everyone = seqs * chips * CORES
    partial_score = jnp.broadcast_to(partial_score, (everyone,) + partial_score.shape)
    partial_score, pooled, active = tied(partial_score, pooled, active)
    scores = lax.all_to_all(partial_score, ("seq", "ch"), 0, 0, tiled=True)
    pooled_parts = [pooled[:quarter], pooled[quarter:]]
    pooled_own = choose(strand, pooled_parts) + core_swap(choose(1 - strand, pooled_parts))
    last_active = jnp.dot(active, by_distance, preferred_element_type=f32).astype(bf16)
    wide_columns = jnp.concatenate([half_columns] * 3, axis=1)
    scores, pooled_own, last_active, wide_columns = tied(
        scores, pooled_own, last_active, wide_columns
    )
    actives.append(last_active)
    window_score = jnp.sum(scores, axis=0)
    loss_slope = (jnp.exp(window_score) - targets) / counts

    grad = lax.dot_general(
        jnp.concatenate(pieces((0.5 / WIN * loss_slope)[:, None] * member.astype(f32))),
        wide_columns,
        (((0,), (1,)), ((), ())),
        preferred_element_type=f32,
    )
    sums = []
    pooled_bit = 1
    for layer in reversed(range(LAYERS)):
        upstream = grad.astype(bf16)
        taps = [rolled(upstream, (1 - tap) * reach[layer]) for tap in range(3)]
        back = sum(
            jnp.dot(taps[tap], filters[layer][tap], preferred_element_type=f32)
            for tap in range(3)
        )
        mine, sends = chip_scatter_parts(back, chip, chips)
        sends, taps = tied(sends, taps)
        received = [chip_shift(sent, by) for by, sent in enumerate(sends, 1)]
        for s in sums:
            s.start()
        if pooled_bit < seqs:
            pooled_received = seq_swap(pooled_own, pooled_bit)
            pooled_bit *= 2
        else:
            pooled_received = jnp.zeros_like(pooled_own)
        halves = [
            jnp.concatenate([tap[:, :quarter] for tap in taps], axis=1),
            jnp.concatenate([tap[:, quarter:] for tap in taps], axis=1),
        ]
        theirs = lax.dot_general(
            actives[layer],
            choose(1 - strand, halves),
            (((0,), (0,)), ((), ())),
            preferred_element_type=f32,
        ).astype(bf16)
        theirs = core_swap(theirs)
        ours = choose(strand, halves)
        near, far = jnp.split(actives[layer], 2, axis=1)
        keep = lax.dot_general(
            near, ours, (((0,), (0,)), ((), ())), preferred_element_type=f32
        ) + theirs[: channels // 2].astype(f32)
        send = (
            lax.dot_general(far, ours, (((0,), (0,)), ((), ())), preferred_element_type=f32)
            + theirs[channels // 2 :].astype(f32)
        ).astype(bf16)
        due = [s for s in sums if s.bit > 1 or layer < LAYERS - 1 - s.slot - 1]
        received, due_received, pooled_received, keep, send = tied(
            received, [s.received for s in due], pooled_received, keep, send
        )
        for s, got in zip(due, due_received):
            s.received = got
            s.join()
        pooled_own = pooled_own + pooled_received
        sums.append(BlockSum(keep, send))
        sums[-1].slot = LAYERS - 1 - layer
        through = mine
        for got in received:
            through = through + got.astype(f32)
        pullback = jax.vjp(jax.nn.gelu, streams[layer])[1]
        grad = grad + pullback(through)[0]

    for s in sums:
        s.start()
    stem_part = lax.dot_general(
        grad.astype(bf16), letters, (((0,), (0,)), ((), ())), preferred_element_type=f32
    )
    stem_parts = [stem_part[:quarter], stem_part[quarter:]]
    stem_own = choose(strand, stem_parts) + core_swap(
        choose(1 - strand, stem_parts).astype(bf16)
    ).astype(f32)
    stem_send = stem_own.astype(bf16).reshape(seqs, quarter // seqs, -1)
    stem_blocks = lax.all_to_all(stem_send, "seq", 0, 0, tiled=True)
    stem_blocks, seq_received, pooled_own = tied(
        stem_blocks, [s.received for s in sums], pooled_own
    )
    for s, got in zip(sums, seq_received):
        s.received = got
        if s.bit < seqs // 2:
            s.join()
            s.start()
    stem_block = jnp.sum(stem_blocks.astype(f32), axis=0)
    stem_grad = lax.all_to_all(
        jnp.broadcast_to(stem_block, (seqs,) + stem_block.shape), "seq", 0, 0, tiled=True
    ).reshape(quarter, -1)
    while pooled_bit < seqs:
        pooled_own = pooled_own + seq_swap(pooled_own, pooled_bit)
        pooled_bit *= 2
    head_grad = lax.dot_general(
        jnp.concatenate(pieces(0.5 * loss_slope[None, :] * pooled_own), axis=1),
        jnp.concatenate([at_track] * 3),
        (((1,), (0,)), ((), ())),
        preferred_element_type=f32,
    )
    for s in sums:
        while s.bit < seqs // 2:
            s.join()
            s.start()
    conv_grad = assemble(sums[::-1], quarter)
    return (window_score, conv_grad, stem_grad, head_grad)


def solution(mesh):
    return jax.shard_map(
        shards,
        mesh=mesh,
        in_specs=(
            P("seq", None),
            P("ch", None),
            P(None, None, "ch", None),
            P("ch", None),
            P(),
            P(),
            P(),
        ),
        out_specs=(P(), P(None, None, "ch", "seq"), P("ch", None), P("ch", None)),
        check_vma=False,
    )
```

```python
import jax
import jax.numpy as jnp
from jax import lax
from jax.experimental import pallas as pl
from jax.experimental.pallas import tpu as pltpu
from jax.sharding import PartitionSpec as P

LAYERS = 5
WIN = 16
CORES = 2
VMEM = 12 << 20

bf16 = jnp.bfloat16
f32 = jnp.float32


def dilations(shard_rows):
    return (shard_rows // 8, shard_rows // 2, shard_rows, 2 * shard_rows, 4 * shard_rows)


def core_swap(value):
    count = lax.axis_size("ch")
    return lax.ppermute(value, "ch", [(i, i ^ 1) for i in range(count)])


def chip_shift(value, by):
    count = lax.axis_size("ch")
    return lax.ppermute(value, "ch", [(i, (i + CORES * by) % count) for i in range(count)])


def seq_swap(value, bit):
    count = lax.axis_size("seq")
    return lax.ppermute(value, "seq", [(i, i ^ bit) for i in range(count)])


def choose(index, options):
    picked = options[0]
    for place, option in enumerate(options[1:], 1):
        picked = jnp.where(index == place, option, picked)
    return picked


def rolled(field, by):
    if by == 0:
        return field
    blank = jnp.zeros((abs(by),) + field.shape[1:], field.dtype)
    if by > 0:
        return jnp.concatenate([field[by:], blank], axis=0)
    return jnp.concatenate([blank, field[:by]], axis=0)


def tied(*values):
    return lax.optimization_barrier(values)


def by_strand(strand, own, sibling):
    return [jnp.where(strand == 0, own, sibling), jnp.where(strand == 0, sibling, own)]


def pieces(value):
    high = value.astype(bf16)
    rest = value - high.astype(f32)
    middle = rest.astype(bf16)
    return high, middle, (rest - middle.astype(f32)).astype(bf16)


def run(body, outs, *values, inside=True):
    if not inside:
        return body(jnp.roll, *values)

    def kernel(*refs):
        results = body(pltpu.roll, *[ref[...] for ref in refs[: len(values)]])
        for ref, result in zip(refs[len(values) :], results):
            ref[...] = result

    return pl.pallas_call(
        kernel,
        out_shape=[jax.ShapeDtypeStruct(shape, kind) for shape, kind in outs],
        compiler_params=pltpu.CompilerParams(vmem_limit_bytes=VMEM),
    )(*values)


def moved(roll, field, by):
    if by == 0:
        return field
    rows = field.shape[0]
    row = lax.broadcasted_iota(jnp.int32, field.shape, 0)
    there = (row + by >= 0) & (row + by < rows)
    return jnp.where(there, roll(field, (-by) % rows, 0), 0.0)


def slope_of_gelu(value):
    scale = 0.7978845608028654
    bend = jnp.tanh(scale * (value + 0.044715 * value * value * value))
    return 0.5 * (1.0 + bend) + 0.5 * value * (1.0 - bend * bend) * scale * (
        1.0 + 3 * 0.044715 * value * value
    )


def back_body(reach, chips, first):
    def body(roll, chip, grad, *rest):
        if first:
            (taps,) = rest
        else:
            mine, received, stream, taps = rest
            through = mine
            for part in range(chips - 1):
                through = through + received[part].astype(f32)
            grad = grad + through * slope_of_gelu(stream)
        upstream = grad.astype(bf16)
        wide = upstream.astype(f32)
        fields = [moved(roll, wide, (1 - tap) * reach).astype(bf16) for tap in range(3)]
        back = jnp.dot(
            jnp.concatenate(fields, axis=1),
            taps.reshape(-1, taps.shape[-1]),
            preferred_element_type=f32,
        )
        width = grad.shape[1]
        parts = [back[:, i * width : (i + 1) * width] for i in range(chips)]
        index = chip[0, 0]
        sends = [
            choose((index + by) % chips, parts).astype(bf16)[None] for by in range(1, chips)
        ]
        sends = sends[0] if chips == 2 else jnp.concatenate(sends)
        return grad, upstream, choose(index, parts), sends

    return body


def side_taps(roll, upstream, side, reach, quarter):
    shape = (upstream.shape[1], 3 * quarter)
    source = lax.broadcasted_iota(jnp.int32, shape, 0)
    target = lax.broadcasted_iota(jnp.int32, shape, 1)
    tap = (target >= quarter).astype(jnp.int32) + (target >= 2 * quarter).astype(jnp.int32)
    spread = (source == side * quarter + target - tap * quarter).astype(f32).astype(bf16)
    wide = jnp.dot(upstream, spread, preferred_element_type=f32)
    lane = lax.broadcasted_iota(jnp.int32, wide.shape, 1)
    low, high = moved(roll, wide, reach), moved(roll, wide, -reach)
    return jnp.where(lane < quarter, low, jnp.where(lane < 2 * quarter, wide, high)).astype(bf16)


def filter_theirs(active, upstream, strand, reach, quarter):
    def body(roll, strand, active, upstream):
        taps = side_taps(roll, upstream, 1 - strand[0, 0], reach, quarter)
        return (jnp.dot(active, taps, preferred_element_type=f32).astype(bf16),)

    return run(body, [((active.shape[0], 3 * quarter), bf16)], strand, active, upstream)[0]


def filter_ours(active, upstream, strand, theirs, reach, quarter):
    half = active.shape[0] // 2

    def body(roll, strand, active, upstream, theirs):
        taps = side_taps(roll, upstream, strand[0, 0], reach, quarter)
        keep = jnp.dot(active[:half], taps, preferred_element_type=f32)
        send = jnp.dot(active[half:], taps, preferred_element_type=f32)
        return (
            keep + theirs[:half].astype(f32),
            (send + theirs[half:].astype(f32)).astype(bf16),
        )

    shape = (half, 3 * quarter)
    return run(body, [(shape, f32), (shape, bf16)], strand, active, upstream, theirs)


def last_body(chips, quarter):
    def body(roll, strand, grad, mine, received, stream, letters):
        through = mine
        for part in range(chips - 1):
            through = through + received[part].astype(f32)
        grad = grad + through * slope_of_gelu(stream)
        stem = jnp.dot(grad.T.astype(bf16), letters, preferred_element_type=f32)
        parts = [stem[:quarter], stem[quarter:]]
        return choose(strand[0, 0], parts), choose(1 - strand[0, 0], parts).astype(bf16)

    return body


class BlockSum:
    def __init__(self, kept, sent, slot):
        self.kept, self.sent, self.slot = kept, sent, slot
        self.bit = 1
        self.received = None

    def start(self):
        if self.sent is not None and self.received is None:
            self.received = seq_swap(self.sent, self.bit)

    def last(self):
        return 2 * self.bit >= lax.axis_size("seq")

    def join(self):
        if self.last():
            self.sent = None
            return

        def body(roll, kept, received):
            total = kept + received.astype(f32)
            half = total.shape[0] // 2
            return total[:half], total[half:].astype(bf16)

        shape = (self.kept.shape[0] // 2, self.kept.shape[1])
        self.kept, self.sent = run(body, [(shape, f32), (shape, bf16)], self.kept, self.received)
        self.bit *= 2
        self.received = None


def assemble(sums, quarter):
    block = sums[0].kept.shape[0]
    taps = sums[0].kept.shape[1] // quarter
    count = len(sums)

    def kernel(*refs):
        out = refs[-1]
        for layer in range(count):
            total = refs[layer][...] + refs[count + layer][...].astype(f32)
            out[layer] = total.T.reshape(taps, quarter, block)

    return pl.pallas_call(
        kernel,
        out_shape=jax.ShapeDtypeStruct((count, taps, quarter, block), f32),
        compiler_params=pltpu.CompilerParams(vmem_limit_bytes=VMEM),
    )(*[s.kept for s in sums], *[s.received for s in sums])


def shards(
    genome, stem_weight, dilated_filter_weight, head_weight, window_start, window_track, targets
):
    shard_rows, pool = genome.shape
    seqs = lax.axis_size("seq")
    chips = lax.axis_size("ch") // CORES
    seq = lax.axis_index("seq")
    strand = lax.axis_index("ch") % CORES
    chip = lax.axis_index("ch") // CORES
    spans = dilations(shard_rows)
    classes = spans[0]
    own_classes = classes // seqs
    steps = shard_rows // classes
    reach = tuple(span // classes * own_classes for span in spans)
    quarter = stem_weight.shape[0]
    channels = dilated_filter_weight.shape[3]
    block = channels // seqs
    tracks = head_weight.shape[1]

    blocks = (
        genome.astype(bf16)
        .reshape(steps, seqs, own_classes, pool)
        .transpose(1, 0, 2, 3)
        .reshape(seqs, steps * own_classes, pool)
    )
    blocks = lax.all_to_all(blocks, "seq", 0, 0, tiled=True)

    stem_own = [stem_weight] + [chip_shift(stem_weight, by) for by in range(1, chips)]
    stem_pairs = [
        jnp.concatenate(by_strand(strand, part, core_swap(part))) for part in stem_own
    ]
    stem_full = jnp.concatenate([choose((chip - p) % chips, stem_pairs) for p in range(chips)])

    sibling_filter = core_swap(dilated_filter_weight)

    own_filter = dilated_filter_weight

    def filter_of(layer):
        return jnp.concatenate(
            by_strand(strand, own_filter[layer], sibling_filter[layer]), axis=1
        )

    bases = blocks.reshape(shard_rows, pool)
    row = jnp.arange(shard_rows, dtype=jnp.int32)
    step_of = row // own_classes
    step_of = jnp.where(strand == 0, step_of, shard_rows // own_classes - 1 - step_of)
    class_of = row % own_classes
    source_row = step_of * own_classes + class_of
    order = (source_row[:, None] == row[None, :]).astype(bf16)
    letter = jnp.arange(4 * pool, dtype=jnp.int32)
    place = jnp.where(strand == 0, letter // 4, pool - 1 - letter // 4)
    spread_place = (jnp.arange(pool, dtype=jnp.int32)[:, None] == place[None, :]).astype(bf16)
    base_of = jnp.where(strand == 0, letter % 4, 3 - letter % 4)
    ordered = jnp.dot(order, bases, preferred_element_type=f32).astype(bf16)
    wide = jnp.dot(ordered, spread_place, preferred_element_type=f32)
    letters = (wide == base_of[None, :].astype(f32)).astype(bf16)
    position = step_of * classes + seq * own_classes + class_of

    member = (
        (position[None, :] >= window_start[:, None])
        & (position[None, :] < window_start[:, None] + WIN)
    ).astype(bf16)
    counts = jnp.sum((window_track[:, None] == window_track[None, :]).astype(f32), axis=1)
    at_track = (
        jnp.arange(tracks, dtype=jnp.int32)[None, :] == window_track[:, None]
    ).astype(bf16)

    bits = seqs.bit_length() - 1
    slot = jnp.arange(channels, dtype=jnp.int32) // block
    away = sum(((slot >> (bits - 1 - b)) & 1) << b for b in range(bits))
    wanted = (seq ^ away) * block + jnp.arange(channels, dtype=jnp.int32) % block
    by_distance = (
        jnp.arange(channels, dtype=jnp.int32)[:, None] == wanted[None, :]
    ).astype(bf16)

    whole = lax.dot_general(
        letters, stem_full, (((1,), (1,)), ((), ())), preferred_element_type=f32
    )
    active = jax.nn.gelu(whole).astype(bf16)
    stream = choose(chip, jnp.split(whole, chips, axis=1))
    filters = [filter_of(0)]
    streams = []
    actives = []
    for layer in range(LAYERS):
        streams.append(stream)
        for tap in range(3):
            stream = stream + lax.dot_general(
                rolled(active, (tap - 1) * reach[layer]),
                filters[layer][tap],
                (((1,), (1,)), ((), ())),
                preferred_element_type=f32,
            )
        if layer < LAYERS - 1:
            own = jax.nn.gelu(stream).astype(bf16)
            own, own_filter, sibling_filter, by_distance, at_track = tied(
                own, own_filter, sibling_filter, by_distance, at_track
            )
            parts = [chip_shift(own, by) for by in range(1, chips)]
            beside = [
                filter_of(layer + 1),
                lax.dot_general(
                    by_distance, active, (((0,), (1,)), ((), ())), preferred_element_type=f32
                ).astype(bf16),
            ]
            if layer == 1:
                columns = lax.dot_general(
                    head_weight, at_track, (((1,), (1,)), ((), ())), preferred_element_type=f32
                ).astype(bf16)
                beside.append(columns)
            if layer == 2:
                beside.append(jnp.concatenate(by_strand(strand, columns, core_swap(columns))))
            parts, beside = tied(parts, beside)
            filters.append(beside[0])
            actives.append(beside[1])
            if layer == 1:
                columns = beside[2]
            if layer == 2:
                half_columns = beside[2]
            parts = [own] + list(parts)
            active = jnp.concatenate(
                [choose((chip - p) % chips, parts) for p in range(chips)], axis=1
            )

    pooled = (
        lax.dot_general(
            jnp.concatenate(pieces(stream)),
            jnp.concatenate([member] * 3, axis=1),
            (((0,), (1,)), ((), ())),
            preferred_element_type=f32,
        )
        / WIN
    )
    partial_score = 0.5 * jnp.sum(pooled * half_columns.astype(f32), axis=0)
    everyone = seqs * chips * CORES
    partial_score = jnp.broadcast_to(partial_score, (everyone,) + partial_score.shape)
    partial_score, pooled, active = tied(partial_score, pooled, active)
    scores = lax.all_to_all(partial_score, ("seq", "ch"), 0, 0, tiled=True)
    pooled_parts = [pooled[:quarter], pooled[quarter:]]
    pooled_own = choose(strand, pooled_parts) + core_swap(choose(1 - strand, pooled_parts))
    last_active = lax.dot_general(
        by_distance, active, (((0,), (1,)), ((), ())), preferred_element_type=f32
    ).astype(bf16)
    wide_columns = jnp.concatenate([half_columns] * 3, axis=1)
    scores, pooled_own, last_active, wide_columns = tied(
        scores, pooled_own, last_active, wide_columns
    )
    actives.append(last_active)
    window_score = jnp.sum(scores, axis=0)
    loss_slope = (jnp.exp(window_score) - targets) / counts

    grad = lax.dot_general(
        jnp.concatenate(pieces((0.5 / WIN * loss_slope)[:, None] * member.astype(f32))),
        wide_columns,
        (((0,), (1,)), ((), ())),
        preferred_element_type=f32,
    )
    sums = []
    pooled_bit = 1
    aligned = (channels // chips) % 128 == 0
    shape = (shard_rows, channels // chips)
    back_outs = [(shape, f32), (shape, bf16), (shape, f32), ((chips - 1,) + shape, bf16)]
    chip_word = jnp.reshape(chip, (1, 1))
    strand_word = jnp.reshape(strand, (1, 1))
    state = (grad,)
    for layer in reversed(range(LAYERS)):
        first = layer == LAYERS - 1
        grad, upstream, mine, sends = run(
            back_body(reach[layer], chips, first),
            back_outs,
            chip_word,
            *state,
            filters[layer],
            inside=aligned,
        )
        sends, upstream = tied(sends, upstream)
        received = jnp.stack([chip_shift(sends[by - 1], by) for by in range(1, chips)])
        for s in sums:
            s.start()
        if pooled_bit < seqs:
            pooled_received = seq_swap(pooled_own, pooled_bit)
            pooled_bit *= 2
        else:
            pooled_received = jnp.zeros_like(pooled_own)
        theirs = core_swap(
            filter_theirs(actives[layer], upstream, strand_word, reach[layer], quarter)
        )
        keep, send = filter_ours(
            actives[layer], upstream, strand_word, theirs, reach[layer], quarter
        )
        due = [s for s in sums if s.sent is not None and (s.bit > 1 or layer < LAYERS - 2 - s.slot)]
        received, due_received, pooled_received, keep, send = tied(
            received, [s.received for s in due], pooled_received, keep, send
        )
        for s, got in zip(due, due_received):
            s.received = got
            s.join()
        pooled_own = pooled_own + pooled_received
        sums.append(BlockSum(keep, send, LAYERS - 1 - layer))
        state = (grad, mine, received, streams[layer])

    for s in sums:
        s.start()
    stem_shape = (quarter, letters.shape[1])
    stem_keep, stem_away = run(
        last_body(chips, quarter),
        [(stem_shape, f32), (stem_shape, bf16)],
        strand_word,
        *state,
        letters,
        inside=aligned,
    )
    stem_own = stem_keep + core_swap(stem_away).astype(f32)
    stem_send = stem_own.astype(bf16).reshape(seqs, quarter // seqs, -1)
    stem_blocks = lax.all_to_all(stem_send, "seq", 0, 0, tiled=True)
    stem_blocks, seq_received, pooled_own = tied(
        stem_blocks, [s.received for s in sums], pooled_own
    )
    for s, got in zip(sums, seq_received):
        s.received = got
        if not s.last():
            s.join()
            s.start()
    stem_block = jnp.sum(stem_blocks.astype(f32), axis=0)
    stem_grad = lax.all_to_all(
        jnp.broadcast_to(stem_block, (seqs,) + stem_block.shape), "seq", 0, 0, tiled=True
    ).reshape(quarter, -1)
    while pooled_bit < seqs:
        pooled_own = pooled_own + seq_swap(pooled_own, pooled_bit)
        pooled_bit *= 2
    head_grad = lax.dot_general(
        jnp.concatenate(pieces(0.5 * loss_slope[None, :] * pooled_own), axis=1),
        jnp.concatenate([at_track] * 3),
        (((1,), (0,)), ((), ())),
        preferred_element_type=f32,
    )
    for s in sums:
        while not s.last():
            s.join()
            s.start()
    conv_grad = assemble(sums[::-1], quarter)
    return (window_score, conv_grad, stem_grad, head_grad)


def solution(mesh):
    return jax.shard_map(
        shards,
        mesh=mesh,
        in_specs=(
            P("seq", None),
            P("ch", None),
            P(None, None, "ch", None),
            P("ch", None),
            P(),
            P(),
            P(),
        ),
        out_specs=(P(), P(None, None, "ch", "seq"), P("ch", None), P("ch", None)),
        check_vma=False,
    )
```

```python
import jax
import jax.numpy as jnp
from jax import lax
from jax.experimental import pallas as pl
from jax.experimental.pallas import tpu as pltpu
from jax.sharding import PartitionSpec as P

LAYERS = 5
WIN = 16
CORES = 2
VMEM = 12 << 20

bf16 = jnp.bfloat16
f32 = jnp.float32


def dilations(shard_rows):
    return (shard_rows // 8, shard_rows // 2, shard_rows, 2 * shard_rows, 4 * shard_rows)


def core_swap(value):
    count = lax.axis_size("ch")
    return lax.ppermute(value, "ch", [(i, i ^ 1) for i in range(count)])


def chip_shift(value, by):
    count = lax.axis_size("ch")
    return lax.ppermute(value, "ch", [(i, (i + CORES * by) % count) for i in range(count)])


def seq_swap(value, bit):
    count = lax.axis_size("seq")
    return lax.ppermute(value, "seq", [(i, i ^ bit) for i in range(count)])


def choose(index, options):
    picked = options[0]
    for place, option in enumerate(options[1:], 1):
        picked = jnp.where(index == place, option, picked)
    return picked


def rolled(field, by):
    if by == 0:
        return field
    blank = jnp.zeros((abs(by),) + field.shape[1:], field.dtype)
    if by > 0:
        return jnp.concatenate([field[by:], blank], axis=0)
    return jnp.concatenate([blank, field[:by]], axis=0)


def tied(*values):
    return lax.optimization_barrier(values)


def by_strand(strand, own, sibling):
    return [jnp.where(strand == 0, own, sibling), jnp.where(strand == 0, sibling, own)]


def pieces(value):
    high = value.astype(bf16)
    rest = value - high.astype(f32)
    middle = rest.astype(bf16)
    return high, middle, (rest - middle.astype(f32)).astype(bf16)


def run(body, outs, *values, inside=True):
    if not inside:
        return body(jnp.roll, *values)

    def kernel(*refs):
        results = body(pltpu.roll, *[ref[...] for ref in refs[: len(values)]])
        for ref, result in zip(refs[len(values) :], results):
            ref[...] = result

    return pl.pallas_call(
        kernel,
        out_shape=[jax.ShapeDtypeStruct(shape, kind) for shape, kind in outs],
        compiler_params=pltpu.CompilerParams(vmem_limit_bytes=VMEM),
        cost_estimate=pl.CostEstimate(flops=1, bytes_accessed=1, transcendentals=0),
    )(*values)


def moved(roll, field, by):
    if by == 0:
        return field
    rows = field.shape[0]
    row = lax.broadcasted_iota(jnp.int32, field.shape, 0)
    there = (row + by >= 0) & (row + by < rows)
    return jnp.where(there, roll(field, (-by) % rows, 0), 0.0)


def slope_of_gelu(value):
    scale = 0.7978845608028654
    bend = jnp.tanh(scale * (value + 0.044715 * value * value * value))
    return 0.5 * (1.0 + bend) + 0.5 * value * (1.0 - bend * bend) * scale * (
        1.0 + 3 * 0.044715 * value * value
    )


def back_body(reach, chips, quarter, first):
    def body(roll, chip, strand, grad, *rest):
        if first:
            (taps,) = rest
        else:
            mine, received, stream, taps = rest
            through = mine
            for part in range(chips - 1):
                through = through + received[part].astype(f32)
            grad = grad + through * slope_of_gelu(stream)
        upstream = grad.astype(bf16)
        wide = upstream.astype(f32)
        fields = [moved(roll, wide, (1 - tap) * reach).astype(bf16) for tap in range(3)]
        back = jnp.dot(
            jnp.concatenate(fields, axis=1),
            taps.reshape(-1, taps.shape[-1]),
            preferred_element_type=f32,
        )
        width = grad.shape[1]
        parts = [back[:, i * width : (i + 1) * width] for i in range(chips)]
        index = chip[0, 0]
        sends = [
            choose((index + by) % chips, parts).astype(bf16)[None] for by in range(1, chips)
        ]
        sends = sends[0] if chips == 2 else jnp.concatenate(sends)
        source = lax.broadcasted_iota(jnp.int32, (width, quarter), 0)
        target = lax.broadcasted_iota(jnp.int32, (width, quarter), 1)
        theirs = (source == target + (1 - strand[0, 0]) * quarter).astype(f32).astype(bf16)
        theirs = jnp.dot(upstream, theirs, preferred_element_type=f32).astype(bf16)
        return grad, upstream, choose(index, parts), sends, theirs

    return body


def score_body(quarter, everyone):
    def body(roll, strand, stream, member, columns):
        pooled = sum(
            jnp.dot(term, member, preferred_element_type=f32) for term in pieces(stream.T)
        ) / WIN
        partial = 0.5 * jnp.sum(pooled * columns.astype(f32), axis=0, keepdims=True)
        parts = [pooled[:quarter], pooled[quarter:]]
        return (
            jnp.broadcast_to(partial, (everyone, partial.shape[1])),
            choose(strand[0, 0], parts),
            choose(1 - strand[0, 0], parts),
        )

    return body


def loss_body(reach, chips, quarter):
    back = back_body(reach, chips, quarter, True)

    def body(roll, chip, strand, scores, targets, counts, member, columns, taps):
        score = jnp.sum(scores, axis=0, keepdims=True)
        slope = (jnp.exp(score) - targets) / counts
        grad = sum(
            lax.dot_general(
                term, columns, (((1,), (1,)), ((), ())), preferred_element_type=f32
            )
            for term in pieces(0.5 / WIN * slope * member.astype(f32))
        )
        return (score, slope, *back(roll, chip, strand, grad, taps))

    return body


def genome_body(steps, seqs, own_classes):
    def body(roll, genome):
        rows = genome.shape[0]
        target = lax.broadcasted_iota(jnp.int32, (rows, rows), 0)
        source = lax.broadcasted_iota(jnp.int32, (rows, rows), 1)
        owner, local = target // (steps * own_classes), target % (steps * own_classes)
        step, kind = local // own_classes, local % own_classes
        wanted = step * (seqs * own_classes) + owner * own_classes + kind
        order = (source == wanted).astype(f32).astype(bf16)
        bases = genome.astype(f32).astype(bf16)
        return (jnp.dot(order, bases, preferred_element_type=f32).astype(bf16),)

    return body


def stem(strand, chip, bases, quarters, chips, own_classes):
    rows, pool = bases.shape
    quarter = quarters[0].shape[0]
    width = chips * CORES * quarter

    def kernel(strand_ref, chip_ref, bases_ref, *refs):
        letters_ref, active_ref, stream_ref, weight_ref = refs[len(quarters) :]
        strand, chip = strand_ref[0, 0], chip_ref[0, 0]
        for by in range(chips):
            for core in range(CORES):
                at = (chip + chips - by) % chips * CORES + (strand + core) % CORES
                weight_ref[pl.ds(at * quarter, quarter), :] = refs[by * CORES + core][...]
        target = lax.broadcasted_iota(jnp.int32, (rows, rows), 0)
        source = lax.broadcasted_iota(jnp.int32, (rows, rows), 1)
        step = target // own_classes
        step = jnp.where(strand == 0, step, rows // own_classes - 1 - step)
        order = (source == step * own_classes + target % own_classes).astype(f32).astype(bf16)
        position = lax.broadcasted_iota(jnp.int32, (pool, 4 * pool), 0)
        letter = lax.broadcasted_iota(jnp.int32, (pool, 4 * pool), 1)
        place = jnp.where(strand == 0, letter // 4, pool - 1 - letter // 4)
        spread = (position == place).astype(f32).astype(bf16)
        ordered = jnp.dot(order, bases_ref[...], preferred_element_type=f32).astype(bf16)
        wide = jnp.dot(ordered, spread, preferred_element_type=f32)
        letter = lax.broadcasted_iota(jnp.int32, (rows, 4 * pool), 1) % 4
        base = jnp.where(strand == 0, letter, 3 - letter).astype(f32)
        letters = (wide == base).astype(f32).astype(bf16)
        letters_ref[...] = letters
        whole = lax.dot_general(
            letters, weight_ref[...], (((1,), (1,)), ((), ())), preferred_element_type=f32
        )
        active_ref[...] = jax.nn.gelu(whole).astype(bf16)
        each = width // chips
        stream_ref[...] = choose(chip, [whole[:, i * each : (i + 1) * each] for i in range(chips)])

    return pl.pallas_call(
        kernel,
        out_shape=[
            jax.ShapeDtypeStruct((rows, 4 * pool), bf16),
            jax.ShapeDtypeStruct((rows, width), bf16),
            jax.ShapeDtypeStruct((rows, width // chips), f32),
        ],
        in_specs=[pl.BlockSpec(memory_space=pltpu.SMEM)] * 2
        + [pl.BlockSpec(memory_space=pltpu.VMEM)] * (1 + len(quarters)),
        scratch_shapes=[pltpu.VMEM((width, 4 * pool), bf16)],
        compiler_params=pltpu.CompilerParams(vmem_limit_bytes=VMEM),
        cost_estimate=pl.CostEstimate(flops=1, bytes_accessed=1, transcendentals=0),
    )(strand, chip, bases, *quarters)


def join_filters(strand, own, sibling, layer):
    taps, quarter, channels = own.shape[1:]

    def kernel(strand_ref, own_ref, sibling_ref, out_ref, sems):
        copies = [
            pltpu.make_async_copy(
                ref.at[layer], out_ref.at[:, pl.ds(at * quarter, quarter), :], sems.at[core]
            )
            for core, (ref, at) in enumerate(
                [(own_ref, strand_ref[0, 0]), (sibling_ref, 1 - strand_ref[0, 0])]
            )
        ]
        for copy in copies:
            copy.start()
        for copy in copies:
            copy.wait()

    return pl.pallas_call(
        kernel,
        out_shape=jax.ShapeDtypeStruct((taps, CORES * quarter, channels), bf16),
        in_specs=[
            pl.BlockSpec(memory_space=pltpu.SMEM),
            pl.BlockSpec(memory_space=pl.ANY),
            pl.BlockSpec(memory_space=pl.ANY),
        ],
        out_specs=pl.BlockSpec(memory_space=pl.ANY),
        scratch_shapes=[pltpu.SemaphoreType.DMA((CORES,))],
        compiler_params=pltpu.CompilerParams(vmem_limit_bytes=VMEM),
        cost_estimate=pl.CostEstimate(flops=1, bytes_accessed=1, transcendentals=0),
    )(strand, own, sibling)


def placed(order, active):
    def body(roll, order, active):
        return (
            lax.dot_general(
                order, active, (((1,), (1,)), ((), ())), preferred_element_type=f32
            ).astype(bf16),
        )

    return run(body, [((order.shape[0], active.shape[0]), bf16)], order, active)[0]


def tap_rows(roll, upstream, offset, reach, quarter):
    width = 3 * quarter
    shape = (upstream.shape[1], 2 * width)
    source = lax.broadcasted_iota(jnp.int32, shape, 0)
    target = lax.broadcasted_iota(jnp.int32, shape, 1)
    target = jnp.where(target >= width, target - width, target)
    tap = (target >= quarter).astype(jnp.int32) + (target >= 2 * quarter).astype(jnp.int32)
    spread = (source == offset + target - tap * quarter).astype(f32).astype(bf16)
    wide = jnp.dot(upstream, spread, preferred_element_type=f32)
    lane = lax.broadcasted_iota(jnp.int32, wide.shape, 1)
    late = lane >= width
    lane = jnp.where(late, lane - width, lane)
    low, high = moved(roll, wide, reach), moved(roll, wide, -reach)
    taps = jnp.where(lane < quarter, low, jnp.where(lane < 2 * quarter, wide, high))
    return [jnp.where(late, 0.0, taps).astype(bf16), jnp.where(late, taps, 0.0).astype(bf16)]


def filter_product(strand, active, upstream, active_sibling, upstream_sibling, reach, quarter):
    half = active.shape[0] // 2
    rows = half // 2

    def body(roll, strand, active, upstream, active_sibling, upstream_sibling):
        fields = [active[:half], active[half:], active_sibling[:half], active_sibling[half:]]
        taps = tap_rows(roll, upstream, strand[0, 0] * quarter, reach, quarter)
        taps = taps + tap_rows(roll, upstream_sibling, 0, reach, quarter)
        total = jnp.dot(
            jnp.concatenate(fields, axis=1), jnp.concatenate(taps), preferred_element_type=f32
        )
        return total[:rows], total[rows:].astype(bf16)

    shape = (rows, 6 * quarter)
    return run(
        body,
        [(shape, f32), (shape, bf16)],
        strand,
        active,
        upstream,
        active_sibling,
        upstream_sibling,
    )


def last_body(chips, quarter):
    def body(roll, strand, grad, mine, received, stream, letters):
        through = mine
        for part in range(chips - 1):
            through = through + received[part].astype(f32)
        grad = grad + through * slope_of_gelu(stream)
        stem = jnp.dot(grad.T.astype(bf16), letters, preferred_element_type=f32)
        parts = [stem[:quarter], stem[quarter:]]
        return choose(strand[0, 0], parts), choose(1 - strand[0, 0], parts).astype(bf16)

    return body


class BlockSum:
    def __init__(self, kept, sent, slot):
        self.kept, self.sent, self.slot = kept, sent, slot
        self.bit = 1
        self.received = None

    def start(self):
        if self.sent is not None and self.received is None:
            self.received = seq_swap(self.sent, self.bit)

    def last(self):
        return 2 * self.bit >= lax.axis_size("seq")

    def join(self):
        rows, width = self.kept.shape
        axis = 1 if 4 * self.bit >= lax.axis_size("seq") else 0
        half = (rows, width // 2) if axis else (rows // 2, width)

        def body(roll, kept, received):
            total = kept + received.astype(f32)
            if axis:
                return total[:, : half[1]], total[:, half[1] :].astype(bf16)
            return total[: half[0]], total[half[0] :].astype(bf16)

        self.kept, self.sent = run(body, [(half, f32), (half, bf16)], self.kept, self.received)
        self.bit *= 2
        self.received = None


def settle(sums, value):
    value, received = tied(value, [s.received for s in sums])
    for s, got in zip(sums, received):
        s.received = got
        s.join()
        s.start()
    return value


def assemble(sums, quarter):
    block = sums[0].kept.shape[0]
    taps = sums[0].kept.shape[1] // quarter
    count = len(sums)

    def kernel(*refs):
        out = refs[-1]
        for layer in range(count):
            total = refs[layer][...] + refs[count + layer][...].astype(f32)
            out[layer] = total.T.reshape(taps, quarter, block)

    return pl.pallas_call(
        kernel,
        out_shape=jax.ShapeDtypeStruct((count, taps, quarter, block), f32),
        compiler_params=pltpu.CompilerParams(vmem_limit_bytes=VMEM),
    )(*[s.kept for s in sums], *[s.received for s in sums])


def shards(
    genome, stem_weight, dilated_filter_weight, head_weight, window_start, window_track, targets
):
    shard_rows, pool = genome.shape
    seqs = lax.axis_size("seq")
    chips = lax.axis_size("ch") // CORES
    seq = lax.axis_index("seq")
    strand = lax.axis_index("ch") % CORES
    chip = lax.axis_index("ch") // CORES
    spans = dilations(shard_rows)
    classes = spans[0]
    own_classes = classes // seqs
    steps = shard_rows // classes
    reach = tuple(span // classes * own_classes for span in spans)
    quarter = stem_weight.shape[0]
    channels = dilated_filter_weight.shape[3]
    block = channels // seqs
    tracks = head_weight.shape[1]

    chip_word = jnp.reshape(chip, (1, 1))
    strand_word = jnp.reshape(strand, (1, 1))

    stem_own = [stem_weight] + [chip_shift(stem_weight, by) for by in range(1, chips)]
    quarters = [part for own in stem_own for part in (own, core_swap(own))]

    (blocks,) = run(
        genome_body(steps, seqs, own_classes), [((shard_rows, pool), bf16)], genome
    )
    blocks = lax.all_to_all(
        blocks.reshape(seqs, steps * own_classes, pool), "seq", 0, 0, tiled=True
    )

    sibling_filter = core_swap(dilated_filter_weight)

    own_filter = dilated_filter_weight

    def filter_of(layer):
        return join_filters(strand_word, own_filter, sibling_filter, layer)

    letters, active, stream = stem(
        strand_word, chip_word, blocks.reshape(shard_rows, pool), quarters, chips, own_classes
    )
    row = jnp.arange(shard_rows, dtype=jnp.int32)
    step_of = row // own_classes
    step_of = jnp.where(strand == 0, step_of, shard_rows // own_classes - 1 - step_of)
    class_of = row % own_classes
    position = step_of * classes + seq * own_classes + class_of

    member = (
        (position[:, None] >= window_start[None, :])
        & (position[:, None] < window_start[None, :] + WIN)
    ).astype(bf16)
    counts = jnp.sum((window_track[:, None] == window_track[None, :]).astype(f32), axis=1)
    at_track = (
        jnp.arange(tracks, dtype=jnp.int32)[None, :] == window_track[:, None]
    ).astype(bf16)

    bits = seqs.bit_length() - 1
    slot = jnp.arange(channels, dtype=jnp.int32) // block
    away = (slot >> (bits - 1)) << (bits - 1)
    for b in range(bits - 1):
        away = away + (((slot >> (bits - 2 - b)) & 1) << b)
    wanted = (seq ^ away) * block + jnp.arange(channels, dtype=jnp.int32) % block
    by_distance = (
        wanted[:, None] == jnp.arange(channels, dtype=jnp.int32)[None, :]
    ).astype(bf16)

    filters = [filter_of(0)]
    streams = []
    actives = []
    sibling_actives = []
    for layer in range(LAYERS):
        streams.append(stream)
        for tap in range(3):
            stream = stream + lax.dot_general(
                rolled(active, (tap - 1) * reach[layer]),
                filters[layer][tap],
                (((1,), (1,)), ((), ())),
                preferred_element_type=f32,
            )
        if layer < LAYERS - 1:
            own = jax.nn.gelu(stream).astype(bf16)
            own, own_filter, sibling_filter, by_distance, at_track = tied(
                own, own_filter, sibling_filter, by_distance, at_track
            )
            parts = [chip_shift(own, by) for by in range(1, chips)]
            beside = [
                filter_of(layer + 1),
                placed(by_distance, active),
            ]
            if layer == 1:
                columns = lax.dot_general(
                    head_weight, at_track, (((1,), (1,)), ((), ())), preferred_element_type=f32
                ).astype(bf16)
                beside.append(columns)
            if layer == 2:
                beside.append(jnp.concatenate(by_strand(strand, columns, core_swap(columns))))
            if layer > 0:
                beside.append(core_swap(actives[-1]))
            parts, beside = tied(parts, beside)
            filters.append(beside[0])
            actives.append(beside[1])
            if layer > 0:
                sibling_actives.append(beside[-1])
            if layer == 1:
                columns = beside[2]
            if layer == 2:
                half_columns = beside[2]
            parts = [own] + list(parts)
            active = jnp.concatenate(
                [choose((chip - p) % chips, parts) for p in range(chips)], axis=1
            )

    windows = window_start.shape[0]
    everyone = seqs * chips * CORES
    partial_score, pooled_own, pooled_sent = run(
        score_body(quarter, everyone),
        [((everyone, windows), f32), ((quarter, windows), f32), ((quarter, windows), f32)],
        strand_word,
        stream,
        member,
        half_columns,
    )
    scores = lax.all_to_all(partial_score[:, None], ("seq", "ch"), 0, 0, tiled=True)
    pooled_own = pooled_own + core_swap(pooled_sent)
    pooled_bit = 1
    if pooled_bit < seqs:
        pooled_own = pooled_own + seq_swap(pooled_own, pooled_bit)
        pooled_bit *= 2
    last_active = placed(by_distance, active)
    sibling_active = core_swap(actives[-1])
    scores, pooled_own, last_active, sibling_active = tied(
        scores, pooled_own, last_active, sibling_active
    )
    actives.append(last_active)
    sibling_actives.append(sibling_active)
    sibling_actives.append(core_swap(last_active))

    sums = []
    aligned = (channels // chips) % 128 == 0
    shape = (shard_rows, channels // chips)
    back_outs = [
        (shape, f32),
        (shape, bf16),
        (shape, f32),
        ((chips - 1,) + shape, bf16),
        ((shard_rows, quarter), bf16),
    ]
    state = ()
    for layer in reversed(range(LAYERS)):
        first = layer == LAYERS - 1
        if first:
            window_score, loss_slope, grad, upstream, mine, sends, theirs = run(
                loss_body(reach[layer], chips, quarter),
                [((1, windows), f32)] * 2 + back_outs,
                chip_word,
                strand_word,
                scores[:, 0],
                targets[None],
                counts[None],
                member,
                half_columns,
                filters[layer],
                inside=aligned,
            )
        else:
            grad, upstream, mine, sends, theirs = run(
                back_body(reach[layer], chips, quarter, False),
                back_outs,
                chip_word,
                strand_word,
                *state,
                filters[layer],
                inside=aligned,
            )
        received = jnp.stack([chip_shift(sends[by - 1], by) for by in range(1, chips)])
        upstream = settle(
            [s for s in sums if not s.last() and s.slot < LAYERS - 2 - layer], upstream
        )
        if pooled_bit < seqs:
            pooled_received = seq_swap(pooled_own, pooled_bit)
            pooled_bit *= 2
        else:
            pooled_received = jnp.zeros_like(pooled_own)
        keep, send = filter_product(
            strand_word,
            actives[layer],
            upstream,
            sibling_actives[layer],
            core_swap(theirs),
            reach[layer],
            quarter,
        )
        received, pooled_received, keep, send = tied(received, pooled_received, keep, send)
        pooled_own = pooled_own + pooled_received
        sums.append(BlockSum(keep, send, LAYERS - 1 - layer))
        sums[-1].start()
        state = (grad, mine, received, streams[layer])

    stem_shape = (quarter, letters.shape[1])
    stem_keep, stem_away = run(
        last_body(chips, quarter),
        [(stem_shape, f32), (stem_shape, bf16)],
        strand_word,
        *state,
        letters,
        inside=aligned,
    )
    stem_own = stem_keep + core_swap(stem_away).astype(f32)
    stem_send = stem_own.astype(bf16).reshape(seqs, quarter // seqs, -1)
    stem_send = settle([s for s in sums if not s.last() and s.slot < LAYERS - 1], stem_send)
    stem_blocks = lax.all_to_all(stem_send, "seq", 0, 0, tiled=True)
    stem_blocks = settle([s for s in sums if not s.last() and s.slot < LAYERS - 1], stem_blocks)
    stem_block = jnp.sum(stem_blocks.astype(f32), axis=0)
    stem_grad = lax.all_to_all(
        jnp.broadcast_to(stem_block, (seqs,) + stem_block.shape), "seq", 0, 0, tiled=True
    ).reshape(quarter, -1)
    while pooled_bit < seqs:
        pooled_own = pooled_own + seq_swap(pooled_own, pooled_bit)
        pooled_bit *= 2
    head_grad = lax.dot_general(
        jnp.concatenate(pieces(0.5 * loss_slope * pooled_own), axis=1),
        jnp.concatenate([at_track] * 3),
        (((1,), (0,)), ((), ())),
        preferred_element_type=f32,
    )
    while any(not s.last() for s in sums):
        for s in sums:
            if not s.last():
                s.join()
                s.start()
    conv_grad = assemble(sums[::-1], quarter)
    return (window_score[0], conv_grad, stem_grad, head_grad)


def solution(mesh):
    return jax.shard_map(
        shards,
        mesh=mesh,
        in_specs=(
            P("seq", None),
            P("ch", None),
            P(None, None, "ch", None),
            P("ch", None),
            P(),
            P(),
            P(),
        ),
        out_specs=(P(), P(None, None, "ch", "seq"), P("ch", None), P("ch", None)),
        check_vma=False,
    )
```

```python
import jax
import jax.numpy as jnp
from jax import lax
from jax.experimental import pallas as pl
from jax.experimental.pallas import tpu as pltpu
from jax.sharding import PartitionSpec as P

LAYERS = 5
WIN = 16
CORES = 2
VMEM = 12 << 20
DUE = (("middle2", "middle3", "end4"), ("middle3", "middle4", "summed"), ("middle4", "end4", "summed"), ("end4", "summed", "needed"), ("summed", "needed", "needed"))
POOLED_DUE = ("sent", "summed")
HIGH_FIRST = (1, 0, 0, 0, 0)

bf16 = jnp.bfloat16
f32 = jnp.float32


def dilations(shard_rows):
    return (shard_rows // 8, shard_rows // 2, shard_rows, 2 * shard_rows, 4 * shard_rows)


def core_swap(value):
    count = lax.axis_size("ch")
    return lax.ppermute(value, "ch", [(i, i ^ 1) for i in range(count)])


def chip_shift(value, by):
    count = lax.axis_size("ch")
    return lax.ppermute(value, "ch", [(i, (i + CORES * by) % count) for i in range(count)])


def seq_swap(value, bit):
    count = lax.axis_size("seq")
    return lax.ppermute(value, "seq", [(i, i ^ bit) for i in range(count)])


def choose(index, options):
    picked = options[0]
    for place, option in enumerate(options[1:], 1):
        picked = jnp.where(index == place, option, picked)
    return picked


def rolled(field, by):
    if by == 0:
        return field
    blank = jnp.zeros((abs(by),) + field.shape[1:], field.dtype)
    if by > 0:
        return jnp.concatenate([field[by:], blank], axis=0)
    return jnp.concatenate([blank, field[:by]], axis=0)


def tied(*values):
    return lax.optimization_barrier(values)


def by_strand(strand, own, sibling):
    return [jnp.where(strand == 0, own, sibling), jnp.where(strand == 0, sibling, own)]


def pieces(value):
    high = value.astype(bf16)
    rest = value - high.astype(f32)
    middle = rest.astype(bf16)
    return high, middle, (rest - middle.astype(f32)).astype(bf16)


def run(body, outs, *values, inside=True):
    if not inside:
        return body(jnp.roll, *values)

    def kernel(*refs):
        results = body(pltpu.roll, *[ref[...] for ref in refs[: len(values)]])
        for ref, result in zip(refs[len(values) :], results):
            ref[...] = result

    return pl.pallas_call(
        kernel,
        out_shape=[jax.ShapeDtypeStruct(shape, kind) for shape, kind in outs],
        compiler_params=pltpu.CompilerParams(vmem_limit_bytes=VMEM),
        cost_estimate=pl.CostEstimate(flops=1, bytes_accessed=1, transcendentals=0),
    )(*values)


def moved(roll, field, by):
    if by == 0:
        return field
    rows = field.shape[0]
    row = lax.broadcasted_iota(jnp.int32, field.shape, 0)
    there = (row + by >= 0) & (row + by < rows)
    return jnp.where(there, roll(field, (-by) % rows, 0), 0.0)


def slope_of_gelu(value):
    scale = 0.7978845608028654
    bend = jnp.tanh(scale * (value + 0.044715 * value * value * value))
    return 0.5 * (1.0 + bend) + 0.5 * value * (1.0 - bend * bend) * scale * (
        1.0 + 3 * 0.044715 * value * value
    )


def back_body(reach, chips, quarter, first):
    def body(roll, chip, strand, grad, *rest):
        if first:
            (taps,) = rest
        else:
            mine, received, stream, taps = rest
            through = mine
            for part in range(chips - 1):
                through = through + received[part].astype(f32)
            grad = grad + through * slope_of_gelu(stream)
        upstream = grad.astype(bf16)
        wide = upstream.astype(f32)
        fields = [moved(roll, wide, (1 - tap) * reach).astype(bf16) for tap in range(3)]
        back = jnp.dot(
            jnp.concatenate(fields, axis=1),
            taps.reshape(-1, taps.shape[-1]),
            preferred_element_type=f32,
        )
        width = grad.shape[1]
        parts = [back[:, i * width : (i + 1) * width] for i in range(chips)]
        index = chip[0, 0]
        sends = [
            choose((index + by) % chips, parts).astype(bf16)[None] for by in range(1, chips)
        ]
        sends = sends[0] if chips == 2 else jnp.concatenate(sends)
        source = lax.broadcasted_iota(jnp.int32, (width, quarter), 0)
        target = lax.broadcasted_iota(jnp.int32, (width, quarter), 1)
        theirs = (source == target + (1 - strand[0, 0]) * quarter).astype(f32).astype(bf16)
        theirs = jnp.dot(upstream, theirs, preferred_element_type=f32).astype(bf16)
        return grad, upstream, choose(index, parts), sends, theirs

    return body


def score_body(quarter, everyone):
    def body(roll, strand, stream, member, columns):
        pooled = sum(
            jnp.dot(term, member, preferred_element_type=f32) for term in pieces(stream.T)
        ) / WIN
        partial = 0.5 * jnp.sum(pooled * columns.astype(f32), axis=0, keepdims=True)
        parts = [pooled[:quarter], pooled[quarter:]]
        return (
            jnp.broadcast_to(partial, (everyone, partial.shape[1])),
            choose(strand[0, 0], parts),
            choose(1 - strand[0, 0], parts),
        )

    return body


def loss_body(reach, chips, quarter):
    back = back_body(reach, chips, quarter, True)

    def body(roll, chip, strand, scores, targets, counts, member, columns, taps):
        score = jnp.sum(scores, axis=0, keepdims=True)
        slope = (jnp.exp(score) - targets) / counts
        grad = sum(
            lax.dot_general(
                term, columns, (((1,), (1,)), ((), ())), preferred_element_type=f32
            )
            for term in pieces(0.5 / WIN * slope * member.astype(f32))
        )
        return (score, slope, *back(roll, chip, strand, grad, taps))

    return body


def genome_body(steps, seqs, own_classes):
    def body(roll, genome):
        rows = genome.shape[0]
        target = lax.broadcasted_iota(jnp.int32, (rows, rows), 0)
        source = lax.broadcasted_iota(jnp.int32, (rows, rows), 1)
        owner, local = target // (steps * own_classes), target % (steps * own_classes)
        step, kind = local // own_classes, local % own_classes
        wanted = step * (seqs * own_classes) + owner * own_classes + kind
        order = (source == wanted).astype(f32).astype(bf16)
        bases = genome.astype(f32).astype(bf16)
        return (jnp.dot(order, bases, preferred_element_type=f32).astype(bf16),)

    return body


def stem(strand, chip, bases, quarters, chips, own_classes):
    rows, pool = bases.shape
    quarter = quarters[0].shape[0]
    width = chips * CORES * quarter

    def kernel(strand_ref, chip_ref, bases_ref, *refs):
        letters_ref, active_ref, stream_ref, weight_ref = refs[len(quarters) :]
        strand, chip = strand_ref[0, 0], chip_ref[0, 0]
        for by in range(chips):
            for core in range(CORES):
                at = (chip + chips - by) % chips * CORES + (strand + core) % CORES
                weight_ref[pl.ds(at * quarter, quarter), :] = refs[by * CORES + core][...]
        target = lax.broadcasted_iota(jnp.int32, (rows, rows), 0)
        source = lax.broadcasted_iota(jnp.int32, (rows, rows), 1)
        step = target // own_classes
        step = jnp.where(strand == 0, step, rows // own_classes - 1 - step)
        order = (source == step * own_classes + target % own_classes).astype(f32).astype(bf16)
        position = lax.broadcasted_iota(jnp.int32, (pool, 4 * pool), 0)
        letter = lax.broadcasted_iota(jnp.int32, (pool, 4 * pool), 1)
        place = jnp.where(strand == 0, letter // 4, pool - 1 - letter // 4)
        spread = (position == place).astype(f32).astype(bf16)
        ordered = jnp.dot(order, bases_ref[...], preferred_element_type=f32).astype(bf16)
        wide = jnp.dot(ordered, spread, preferred_element_type=f32)
        letter = lax.broadcasted_iota(jnp.int32, (rows, 4 * pool), 1) % 4
        base = jnp.where(strand == 0, letter, 3 - letter).astype(f32)
        letters = (wide == base).astype(f32).astype(bf16)
        letters_ref[...] = letters
        whole = lax.dot_general(
            letters, weight_ref[...], (((1,), (1,)), ((), ())), preferred_element_type=f32
        )
        active_ref[...] = jax.nn.gelu(whole).astype(bf16)
        each = width // chips
        stream_ref[...] = choose(chip, [whole[:, i * each : (i + 1) * each] for i in range(chips)])

    return pl.pallas_call(
        kernel,
        out_shape=[
            jax.ShapeDtypeStruct((rows, 4 * pool), bf16),
            jax.ShapeDtypeStruct((rows, width), bf16),
            jax.ShapeDtypeStruct((rows, width // chips), f32),
        ],
        in_specs=[pl.BlockSpec(memory_space=pltpu.SMEM)] * 2
        + [pl.BlockSpec(memory_space=pltpu.VMEM)] * (1 + len(quarters)),
        scratch_shapes=[pltpu.VMEM((width, 4 * pool), bf16)],
        compiler_params=pltpu.CompilerParams(vmem_limit_bytes=VMEM),
        cost_estimate=pl.CostEstimate(flops=1, bytes_accessed=1, transcendentals=0),
    )(strand, chip, bases, *quarters)


def join_filters(strand, own, sibling, layer):
    taps, quarter, channels = own.shape[1:]

    def kernel(strand_ref, own_ref, sibling_ref, out_ref, sems):
        copies = [
            pltpu.make_async_copy(
                ref.at[layer], out_ref.at[:, pl.ds(at * quarter, quarter), :], sems.at[core]
            )
            for core, (ref, at) in enumerate(
                [(own_ref, strand_ref[0, 0]), (sibling_ref, 1 - strand_ref[0, 0])]
            )
        ]
        for copy in copies:
            copy.start()
        for copy in copies:
            copy.wait()

    return pl.pallas_call(
        kernel,
        out_shape=jax.ShapeDtypeStruct((taps, CORES * quarter, channels), bf16),
        in_specs=[
            pl.BlockSpec(memory_space=pltpu.SMEM),
            pl.BlockSpec(memory_space=pl.ANY),
            pl.BlockSpec(memory_space=pl.ANY),
        ],
        out_specs=pl.BlockSpec(memory_space=pl.ANY),
        scratch_shapes=[pltpu.SemaphoreType.DMA((CORES,))],
        compiler_params=pltpu.CompilerParams(vmem_limit_bytes=VMEM),
        cost_estimate=pl.CostEstimate(flops=1, bytes_accessed=1, transcendentals=0),
    )(strand, own, sibling)


def placed(order, active):
    def body(roll, order, active):
        return (
            lax.dot_general(
                order, active, (((1,), (1,)), ((), ())), preferred_element_type=f32
            ).astype(bf16),
        )

    return run(body, [((order.shape[0], active.shape[0]), bf16)], order, active)[0]


def tap_rows(roll, upstream, offset, reach, quarter):
    width = 3 * quarter
    shape = (upstream.shape[1], 2 * width)
    source = lax.broadcasted_iota(jnp.int32, shape, 0)
    target = lax.broadcasted_iota(jnp.int32, shape, 1)
    target = jnp.where(target >= width, target - width, target)
    tap = (target >= quarter).astype(jnp.int32) + (target >= 2 * quarter).astype(jnp.int32)
    spread = (source == offset + target - tap * quarter).astype(f32).astype(bf16)
    wide = jnp.dot(upstream, spread, preferred_element_type=f32)
    lane = lax.broadcasted_iota(jnp.int32, wide.shape, 1)
    late = lane >= width
    lane = jnp.where(late, lane - width, lane)
    low, high = moved(roll, wide, reach), moved(roll, wide, -reach)
    taps = jnp.where(lane < quarter, low, jnp.where(lane < 2 * quarter, wide, high))
    return [jnp.where(late, 0.0, taps).astype(bf16), jnp.where(late, taps, 0.0).astype(bf16)]


def filter_product(strand, active, upstream, active_sibling, upstream_sibling, reach, quarter, parts):
    half = active.shape[0] // 2

    def body(roll, strand, active, upstream, active_sibling, upstream_sibling):
        fields = [active[:half], active[half:], active_sibling[:half], active_sibling[half:]]
        taps = tap_rows(roll, upstream, strand[0, 0] * quarter, reach, quarter)
        taps = taps + tap_rows(roll, upstream_sibling, 0, reach, quarter)
        total = jnp.dot(
            jnp.concatenate(fields, axis=1), jnp.concatenate(taps), preferred_element_type=f32
        )
        return parted(total, parts)

    shape = (half // parts, 6 * quarter)
    return run(
        body,
        [(shape, f32)] + [(shape, bf16)] * (parts - 1),
        strand,
        active,
        upstream,
        active_sibling,
        upstream_sibling,
    )


def last_body(chips, quarter):
    def body(roll, strand, grad, mine, received, stream, letters):
        through = mine
        for part in range(chips - 1):
            through = through + received[part].astype(f32)
        grad = grad + through * slope_of_gelu(stream)
        stem = jnp.dot(grad.T.astype(bf16), letters, preferred_element_type=f32)
        parts = [stem[:quarter], stem[quarter:]]
        return choose(strand[0, 0], parts), choose(1 - strand[0, 0], parts).astype(bf16)

    return body


class BlockSum:
    def __init__(self, kept, sends, slot, stages):
        self.kept, self.slot, self.stages = kept, slot, stages
        self.received = self.sent(sends)
        self.done = False

    def sent(self, sends):
        return [seq_swap(part, away) for part, away in zip(sends, distances(self.stages[0])[1:])]

    def last(self):
        return len(self.stages) == 1

    def due(self):
        step = 3 - min(3, len(self.stages))
        return None if self.done else DUE[self.slot][step]

    def join(self):
        self.stages = self.stages[1:]
        parts = len(distances(self.stages[0]))
        rows, width = self.kept.shape
        rows //= parts

        def body(roll, kept, *received):
            total = kept
            for part in received:
                total = total + part.astype(f32)
            return parted(total, parts)

        outs = [((rows, width), f32)] + [((rows, width), bf16)] * (parts - 1)
        self.kept, *sends = run(body, outs, self.kept, *self.received)
        self.received = self.sent(sends)


def distances(bits):
    return [sum(bit for place, bit in enumerate(bits) if (i >> place) & 1) for i in range(1 << len(bits))]


def parted(total, parts):
    rows = total.shape[0] // parts
    pieces_of = [total[i * rows : (i + 1) * rows] for i in range(parts)]
    return [pieces_of[0]] + [piece.astype(bf16) for piece in pieces_of[1:]]


def settle(sums, value, point):
    due = [s for s in sums if s.due() == point]
    value, received = tied(value, [s.received for s in due])
    for s, got in zip(due, received):
        s.received = got
        if s.last():
            s.done = True
        else:
            s.join()
    return value


def assemble(sums, quarter):
    count = len(sums)
    each = 1 + len(sums[0].received)
    half, width = sums[0].kept.shape
    shape = (3, quarter, 2 * half)

    def kernel(*refs):
        out = refs[-1]
        for layer in range(count):
            total = refs[each * layer][...]
            for part in range(1, each):
                total = total + refs[each * layer + part][...].astype(f32)
            total = jnp.concatenate([total[:, : width // 2], total[:, width // 2 :]])
            out[layer] = total.T.reshape(shape)

    return pl.pallas_call(
        kernel,
        out_shape=jax.ShapeDtypeStruct((count,) + shape, f32),
        compiler_params=pltpu.CompilerParams(vmem_limit_bytes=VMEM),
        cost_estimate=pl.CostEstimate(flops=1, bytes_accessed=1, transcendentals=0),
    )(*[value for s in sums for value in [s.kept, *s.received]])


def shards(
    genome, stem_weight, dilated_filter_weight, head_weight, window_start, window_track, targets
):
    shard_rows, pool = genome.shape
    seqs = lax.axis_size("seq")
    chips = lax.axis_size("ch") // CORES
    seq = lax.axis_index("seq")
    strand = lax.axis_index("ch") % CORES
    chip = lax.axis_index("ch") // CORES
    spans = dilations(shard_rows)
    classes = spans[0]
    own_classes = classes // seqs
    steps = shard_rows // classes
    reach = tuple(span // classes * own_classes for span in spans)
    quarter = stem_weight.shape[0]
    channels = dilated_filter_weight.shape[3]
    block = channels // seqs
    tracks = head_weight.shape[1]

    chip_word = jnp.reshape(chip, (1, 1))
    strand_word = jnp.reshape(strand, (1, 1))

    stem_own = [stem_weight] + [chip_shift(stem_weight, by) for by in range(1, chips)]
    quarters = [part for own in stem_own for part in (own, core_swap(own))]

    (blocks,) = run(
        genome_body(steps, seqs, own_classes), [((shard_rows, pool), bf16)], genome
    )
    blocks = lax.all_to_all(
        blocks.reshape(seqs, steps * own_classes, pool), "seq", 0, 0, tiled=True
    )

    sibling_filter = core_swap(dilated_filter_weight)

    own_filter = dilated_filter_weight

    def filter_of(layer):
        return join_filters(strand_word, own_filter, sibling_filter, layer)

    letters, active, stream = stem(
        strand_word, chip_word, blocks.reshape(shard_rows, pool), quarters, chips, own_classes
    )
    row = jnp.arange(shard_rows, dtype=jnp.int32)
    step_of = row // own_classes
    step_of = jnp.where(strand == 0, step_of, shard_rows // own_classes - 1 - step_of)
    class_of = row % own_classes
    position = step_of * classes + seq * own_classes + class_of

    member = (
        (position[:, None] >= window_start[None, :])
        & (position[:, None] < window_start[None, :] + WIN)
    ).astype(bf16)
    counts = jnp.sum((window_track[:, None] == window_track[None, :]).astype(f32), axis=1)
    at_track = (
        jnp.arange(tracks, dtype=jnp.int32)[None, :] == window_track[:, None]
    ).astype(bf16)

    low_first = [(1 << b,) for b in range(seqs.bit_length() - 1)]
    orders = [low_first, low_first[1:] + low_first[:1]]
    place = jnp.arange(channels, dtype=jnp.int32)
    later, local = place // (channels // 2), place % (channels // 2)
    by_distance = []
    for order in orders:
        aways = [0]
        for stage in order:
            aways = [away + far for away in aways for far in distances(stage)]
        away = choose(local // (block // 2), [jnp.full_like(place, away) for away in aways])
        wanted = (seq ^ away) * block + later * (block // 2) + local % (block // 2)
        by_distance.append(
            (wanted[:, None] == jnp.arange(channels, dtype=jnp.int32)[None, :]).astype(bf16)
        )

    filters = [filter_of(0)]
    streams = []
    actives = []
    sibling_actives = []
    for layer in range(LAYERS):
        streams.append(stream)
        for tap in range(3):
            stream = stream + lax.dot_general(
                rolled(active, (tap - 1) * reach[layer]),
                filters[layer][tap],
                (((1,), (1,)), ((), ())),
                preferred_element_type=f32,
            )
        if layer < LAYERS - 1:
            own = jax.nn.gelu(stream).astype(bf16)
            own, own_filter, sibling_filter, by_distance, at_track = tied(
                own, own_filter, sibling_filter, by_distance, at_track
            )
            parts = [chip_shift(own, by) for by in range(1, chips)]
            beside = [
                filter_of(layer + 1),
                placed(by_distance[HIGH_FIRST[LAYERS - 1 - layer]], active),
            ]
            if layer == 1:
                columns = lax.dot_general(
                    head_weight, at_track, (((1,), (1,)), ((), ())), preferred_element_type=f32
                ).astype(bf16)
                beside.append(columns)
            if layer == 2:
                beside.append(jnp.concatenate(by_strand(strand, columns, core_swap(columns))))
            if layer > 0:
                beside.append(core_swap(actives[-1]))
            parts, beside = tied(parts, beside)
            filters.append(beside[0])
            actives.append(beside[1])
            if layer > 0:
                sibling_actives.append(beside[-1])
            if layer == 1:
                columns = beside[2]
            if layer == 2:
                half_columns = beside[2]
            parts = [own] + list(parts)
            active = jnp.concatenate(
                [choose((chip - p) % chips, parts) for p in range(chips)], axis=1
            )

    windows = window_start.shape[0]
    everyone = seqs * chips * CORES
    partial_score, pooled_own, pooled_sent = run(
        score_body(quarter, everyone),
        [((everyone, windows), f32), ((quarter, windows), f32), ((quarter, windows), f32)],
        strand_word,
        stream,
        member,
        half_columns,
    )
    scores = lax.all_to_all(partial_score[:, None], ("seq", "ch"), 0, 0, tiled=True)
    pooled_own = pooled_own + core_swap(pooled_sent)
    pooled_bit = 1
    if pooled_bit < seqs:
        pooled_own = pooled_own + seq_swap(pooled_own.astype(bf16), pooled_bit).astype(f32)
        pooled_bit *= 2
    last_active = placed(by_distance[HIGH_FIRST[0]], active)
    sibling_active = core_swap(actives[-1])
    scores, pooled_own, last_active, sibling_active = tied(
        scores, pooled_own, last_active, sibling_active
    )
    actives.append(last_active)
    sibling_actives.append(sibling_active)
    sibling_actives.append(core_swap(last_active))

    sums = []

    def pooled_step(pooled, value, point):
        total, received, bit, due = pooled
        if not due or due[0] != point:
            return value, pooled
        value, received = tied(value, received)
        total = total + received.astype(f32)
        bit *= 2
        return value, (total, seq_swap(total.astype(bf16), bit) if bit < seqs else None, bit, due[1:])

    pooled = (
        pooled_own,
        seq_swap(pooled_own.astype(bf16), pooled_bit) if pooled_bit < seqs else None,
        pooled_bit,
        POOLED_DUE,
    )
    aligned = (channels // chips) % 128 == 0
    shape = (shard_rows, channels // chips)
    back_outs = [
        (shape, f32),
        (shape, bf16),
        (shape, f32),
        ((chips - 1,) + shape, bf16),
        ((shard_rows, quarter), bf16),
    ]
    state = ()
    for layer in reversed(range(LAYERS)):
        first = layer == LAYERS - 1
        if first:
            window_score, loss_slope, grad, upstream, mine, sends, theirs = run(
                loss_body(reach[layer], chips, quarter),
                [((1, windows), f32)] * 2 + back_outs,
                chip_word,
                strand_word,
                scores[:, 0],
                targets[None],
                counts[None],
                member,
                half_columns,
                filters[layer],
                inside=aligned,
            )
        else:
            grad, upstream, mine, sends, theirs = run(
                back_body(reach[layer], chips, quarter, False),
                back_outs,
                chip_word,
                strand_word,
                *state,
                filters[layer],
                inside=aligned,
            )
        received = jnp.stack([chip_shift(sends[by - 1], by) for by in range(1, chips)])
        slot = LAYERS - 1 - layer
        upstream = settle(sums, upstream, f"middle{slot}")
        kept, *parts = filter_product(
            strand_word,
            actives[layer],
            upstream,
            sibling_actives[layer],
            core_swap(theirs),
            reach[layer],
            quarter,
            2,
        )
        received, kept = tied(received, kept)
        received = settle(sums, received, f"end{slot}")
        received, pooled = pooled_step(pooled, received, f"end{slot}")
        sums.append(BlockSum(kept, parts, slot, orders[HIGH_FIRST[slot]]))
        state = (grad, mine, received, streams[layer])

    stem_shape = (quarter, letters.shape[1])
    stem_keep, stem_away = run(
        last_body(chips, quarter),
        [(stem_shape, f32), (stem_shape, bf16)],
        strand_word,
        *state,
        letters,
        inside=aligned,
    )
    stem_own = stem_keep + core_swap(stem_away).astype(f32)
    stem_send = stem_own.astype(bf16).reshape(seqs, quarter // seqs, -1)
    stem_send = settle(sums, stem_send, "sent")
    stem_send, pooled = pooled_step(pooled, stem_send, "sent")
    stem_blocks = lax.all_to_all(stem_send, "seq", 0, 0, tiled=True)
    stem_blocks = settle(sums, stem_blocks, "summed")
    stem_blocks, pooled = pooled_step(pooled, stem_blocks, "summed")
    stem_block = jnp.sum(stem_blocks.astype(f32), axis=0).astype(bf16)
    stem_grad = lax.all_to_all(
        jnp.broadcast_to(stem_block, (seqs,) + stem_block.shape), "seq", 0, 0, tiled=True
    )
    stem_grad = stem_grad.reshape(quarter, -1).astype(f32)
    pooled_own, received, bit, _ = pooled
    while received is not None:
        pooled_own = pooled_own + received.astype(f32)
        bit *= 2
        received = seq_swap(pooled_own.astype(bf16), bit) if bit < seqs else None
    head_grad = lax.dot_general(
        jnp.concatenate(pieces(0.5 * loss_slope * pooled_own), axis=1),
        jnp.concatenate([at_track] * 3),
        (((1,), (0,)), ((), ())),
        preferred_element_type=f32,
    )
    while any(not s.last() for s in sums):
        for s in sums:
            if not s.last():
                s.join()
    conv_grad = assemble(sums[::-1], quarter)
    return (window_score[0], conv_grad, stem_grad, head_grad)


def solution(mesh):
    return jax.shard_map(
        shards,
        mesh=mesh,
        in_specs=(
            P("seq", None),
            P("ch", None),
            P(None, None, "ch", None),
            P("ch", None),
            P(),
            P(),
            P(),
        ),
        out_specs=(P(), P(None, None, "ch", "seq"), P("ch", None), P("ch", None)),
        check_vma=False,
    )
```

```python
import jax
import jax.numpy as jnp
from jax import lax
from jax.experimental import pallas as pl
from jax.experimental.pallas import tpu as pltpu
from jax.sharding import PartitionSpec as P

LAYERS = 5
WIN = 16
CORES = 2
VMEM = 12 << 20
DUE = (("middle2", "middle3", "end4"), ("middle3", "middle4", "summed"), ("middle4", "end4", "summed"), ("end4", "summed", "needed"), ("end4", "summed", "needed"))
POOLED_DUE = ("sent", "summed")
HIGH_FIRST = (1, 0, 0, 0, 0)

bf16 = jnp.bfloat16
f32 = jnp.float32


def dilations(shard_rows):
    return (shard_rows // 8, shard_rows // 2, shard_rows, 2 * shard_rows, 4 * shard_rows)


def core_swap(value):
    count = lax.axis_size("ch")
    return lax.ppermute(value, "ch", [(i, i ^ 1) for i in range(count)])


def chip_shift(value, by):
    count = lax.axis_size("ch")
    return lax.ppermute(value, "ch", [(i, (i + CORES * by) % count) for i in range(count)])


def seq_swap(value, bit):
    count = lax.axis_size("seq")
    return lax.ppermute(value, "seq", [(i, i ^ bit) for i in range(count)])


def choose(index, options):
    picked = options[0]
    for place, option in enumerate(options[1:], 1):
        picked = jnp.where(index == place, option, picked)
    return picked


def rolled(field, by):
    if by == 0:
        return field
    blank = jnp.zeros((abs(by),) + field.shape[1:], field.dtype)
    if by > 0:
        return jnp.concatenate([field[by:], blank], axis=0)
    return jnp.concatenate([blank, field[:by]], axis=0)


def tied(*values):
    return lax.optimization_barrier(values)


def by_strand(strand, own, sibling):
    return [jnp.where(strand == 0, own, sibling), jnp.where(strand == 0, sibling, own)]


def pieces(value):
    high = value.astype(bf16)
    rest = value - high.astype(f32)
    middle = rest.astype(bf16)
    return high, middle, (rest - middle.astype(f32)).astype(bf16)


def run(body, outs, *values, inside=True):
    if not inside:
        return body(jnp.roll, *values)

    def kernel(*refs):
        results = body(pltpu.roll, *[ref[...] for ref in refs[: len(values)]])
        for ref, result in zip(refs[len(values) :], results):
            ref[...] = result

    return pl.pallas_call(
        kernel,
        out_shape=[jax.ShapeDtypeStruct(shape, kind) for shape, kind in outs],
        compiler_params=pltpu.CompilerParams(vmem_limit_bytes=VMEM),
        cost_estimate=pl.CostEstimate(flops=1, bytes_accessed=1, transcendentals=0),
    )(*values)


def moved(roll, field, by):
    if by == 0:
        return field
    rows = field.shape[0]
    row = lax.broadcasted_iota(jnp.int32, field.shape, 0)
    there = (row + by >= 0) & (row + by < rows)
    return jnp.where(there, roll(field, (-by) % rows, 0), 0.0)


def slope_of_gelu(value):
    scale = 0.7978845608028654
    bend = jnp.tanh(scale * (value + 0.044715 * value * value * value))
    return 0.5 * (1.0 + bend) + 0.5 * value * (1.0 - bend * bend) * scale * (
        1.0 + 3 * 0.044715 * value * value
    )


def back_body(reach, chips, quarter, first):
    def body(roll, chip, strand, grad, *rest):
        if first:
            (taps,) = rest
        else:
            mine, received, stream, taps = rest
            through = mine
            for part in range(chips - 1):
                through = through + received[part].astype(f32)
            grad = grad + through * slope_of_gelu(stream)
        upstream = grad.astype(bf16)
        wide = upstream.astype(f32)
        fields = [moved(roll, wide, (1 - tap) * reach).astype(bf16) for tap in range(3)]
        back = jnp.dot(
            jnp.concatenate(fields, axis=1),
            taps.reshape(-1, taps.shape[-1]),
            preferred_element_type=f32,
        )
        width = grad.shape[1]
        parts = [back[:, i * width : (i + 1) * width] for i in range(chips)]
        index = chip[0, 0]
        sends = [
            choose((index + by) % chips, parts).astype(bf16)[None] for by in range(1, chips)
        ]
        sends = sends[0] if chips == 2 else jnp.concatenate(sends)
        source = lax.broadcasted_iota(jnp.int32, (width, quarter), 0)
        target = lax.broadcasted_iota(jnp.int32, (width, quarter), 1)
        theirs = (source == target + (1 - strand[0, 0]) * quarter).astype(f32).astype(bf16)
        theirs = jnp.dot(upstream, theirs, preferred_element_type=f32).astype(bf16)
        return grad, upstream, choose(index, parts), sends, theirs

    return body


def score_body(quarter, everyone):
    def body(roll, strand, stream, member, columns):
        pooled = sum(
            jnp.dot(term, member, preferred_element_type=f32) for term in pieces(stream.T)
        ) / WIN
        partial = 0.5 * jnp.sum(pooled * columns.astype(f32), axis=0, keepdims=True)
        parts = [pooled[:quarter], pooled[quarter:]]
        return (
            jnp.broadcast_to(partial, (everyone, partial.shape[1])),
            choose(strand[0, 0], parts),
            choose(1 - strand[0, 0], parts),
        )

    return body


def loss_body(reach, chips, quarter):
    back = back_body(reach, chips, quarter, True)

    def body(roll, chip, strand, scores, targets, counts, member, columns, taps):
        score = jnp.sum(scores, axis=0, keepdims=True)
        slope = (jnp.exp(score) - targets) / counts
        grad = sum(
            lax.dot_general(
                term, columns, (((1,), (1,)), ((), ())), preferred_element_type=f32
            )
            for term in pieces(0.5 / WIN * slope * member.astype(f32))
        )
        return (score, slope, *back(roll, chip, strand, grad, taps))

    return body


def genome_body(steps, seqs, own_classes):
    def body(roll, genome):
        rows = genome.shape[0]
        target = lax.broadcasted_iota(jnp.int32, (rows, rows), 0)
        source = lax.broadcasted_iota(jnp.int32, (rows, rows), 1)
        owner, local = target // (steps * own_classes), target % (steps * own_classes)
        step, kind = local // own_classes, local % own_classes
        wanted = step * (seqs * own_classes) + owner * own_classes + kind
        order = (source == wanted).astype(f32).astype(bf16)
        bases = genome.astype(f32).astype(bf16)
        return (jnp.dot(order, bases, preferred_element_type=f32).astype(bf16),)

    return body


def stem(strand, chip, bases, quarters, chips, own_classes):
    rows, pool = bases.shape
    quarter = quarters[0].shape[0]
    width = chips * CORES * quarter

    def kernel(strand_ref, chip_ref, bases_ref, *refs):
        letters_ref, active_ref, stream_ref, weight_ref = refs[len(quarters) :]
        strand, chip = strand_ref[0, 0], chip_ref[0, 0]
        for by in range(chips):
            for core in range(CORES):
                at = (chip + chips - by) % chips * CORES + (strand + core) % CORES
                weight_ref[pl.ds(at * quarter, quarter), :] = refs[by * CORES + core][...]
        target = lax.broadcasted_iota(jnp.int32, (rows, rows), 0)
        source = lax.broadcasted_iota(jnp.int32, (rows, rows), 1)
        step = target // own_classes
        step = jnp.where(strand == 0, step, rows // own_classes - 1 - step)
        order = (source == step * own_classes + target % own_classes).astype(f32).astype(bf16)
        position = lax.broadcasted_iota(jnp.int32, (pool, 4 * pool), 0)
        letter = lax.broadcasted_iota(jnp.int32, (pool, 4 * pool), 1)
        place = jnp.where(strand == 0, letter // 4, pool - 1 - letter // 4)
        spread = (position == place).astype(f32).astype(bf16)
        ordered = jnp.dot(order, bases_ref[...], preferred_element_type=f32).astype(bf16)
        wide = jnp.dot(ordered, spread, preferred_element_type=f32)
        letter = lax.broadcasted_iota(jnp.int32, (rows, 4 * pool), 1) % 4
        base = jnp.where(strand == 0, letter, 3 - letter).astype(f32)
        letters = (wide == base).astype(f32).astype(bf16)
        letters_ref[...] = letters
        whole = lax.dot_general(
            letters, weight_ref[...], (((1,), (1,)), ((), ())), preferred_element_type=f32
        )
        active_ref[...] = jax.nn.gelu(whole).astype(bf16)
        each = width // chips
        stream_ref[...] = choose(chip, [whole[:, i * each : (i + 1) * each] for i in range(chips)])

    return pl.pallas_call(
        kernel,
        out_shape=[
            jax.ShapeDtypeStruct((rows, 4 * pool), bf16),
            jax.ShapeDtypeStruct((rows, width), bf16),
            jax.ShapeDtypeStruct((rows, width // chips), f32),
        ],
        in_specs=[pl.BlockSpec(memory_space=pltpu.SMEM)] * 2
        + [pl.BlockSpec(memory_space=pltpu.VMEM)] * (1 + len(quarters)),
        scratch_shapes=[pltpu.VMEM((width, 4 * pool), bf16)],
        compiler_params=pltpu.CompilerParams(vmem_limit_bytes=VMEM),
        cost_estimate=pl.CostEstimate(flops=1, bytes_accessed=1, transcendentals=0),
    )(strand, chip, bases, *quarters)


def join_filters(strand, own, sibling, layer):
    taps, quarter, channels = own.shape[1:]

    def kernel(strand_ref, own_ref, sibling_ref, out_ref, sems):
        copies = [
            pltpu.make_async_copy(
                ref.at[layer], out_ref.at[:, pl.ds(at * quarter, quarter), :], sems.at[core]
            )
            for core, (ref, at) in enumerate(
                [(own_ref, strand_ref[0, 0]), (sibling_ref, 1 - strand_ref[0, 0])]
            )
        ]
        for copy in copies:
            copy.start()
        for copy in copies:
            copy.wait()

    return pl.pallas_call(
        kernel,
        out_shape=jax.ShapeDtypeStruct((taps, CORES * quarter, channels), bf16),
        in_specs=[
            pl.BlockSpec(memory_space=pltpu.SMEM),
            pl.BlockSpec(memory_space=pltpu.HBM),
            pl.BlockSpec(memory_space=pltpu.HBM),
        ],
        out_specs=pl.BlockSpec(memory_space=pl.ANY),
        scratch_shapes=[pltpu.SemaphoreType.DMA((CORES,))],
        compiler_params=pltpu.CompilerParams(vmem_limit_bytes=VMEM),
        cost_estimate=pl.CostEstimate(flops=1, bytes_accessed=1, transcendentals=0),
    )(strand, own, sibling)


def placed(order, active):
    def body(roll, order, active):
        return (
            lax.dot_general(
                order, active, (((1,), (1,)), ((), ())), preferred_element_type=f32
            ).astype(bf16),
        )

    return run(body, [((order.shape[0], active.shape[0]), bf16)], order, active)[0]


def tap_rows(roll, upstream, offset, reach, quarter):
    width = 3 * quarter
    shape = (upstream.shape[1], 2 * width)
    source = lax.broadcasted_iota(jnp.int32, shape, 0)
    target = lax.broadcasted_iota(jnp.int32, shape, 1)
    target = jnp.where(target >= width, target - width, target)
    tap = (target >= quarter).astype(jnp.int32) + (target >= 2 * quarter).astype(jnp.int32)
    spread = (source == offset + target - tap * quarter).astype(f32).astype(bf16)
    wide = jnp.dot(upstream, spread, preferred_element_type=f32)
    lane = lax.broadcasted_iota(jnp.int32, wide.shape, 1)
    late = lane >= width
    lane = jnp.where(late, lane - width, lane)
    low, high = moved(roll, wide, reach), moved(roll, wide, -reach)
    taps = jnp.where(lane < quarter, low, jnp.where(lane < 2 * quarter, wide, high))
    return [jnp.where(late, 0.0, taps).astype(bf16), jnp.where(late, taps, 0.0).astype(bf16)]


def filter_product(strand, active, upstream, active_sibling, upstream_sibling, reach, quarter, parts):
    half = active.shape[0] // 2

    def body(roll, strand, active, upstream, active_sibling, upstream_sibling):
        fields = [active[:half], active[half:], active_sibling[:half], active_sibling[half:]]
        taps = tap_rows(roll, upstream, strand[0, 0] * quarter, reach, quarter)
        taps = taps + tap_rows(roll, upstream_sibling, 0, reach, quarter)
        total = jnp.dot(
            jnp.concatenate(fields, axis=1), jnp.concatenate(taps), preferred_element_type=f32
        )
        return parted(total, parts)

    shape = (half // parts, 6 * quarter)
    return run(
        body,
        [(shape, f32)] + [(shape, bf16)] * (parts - 1),
        strand,
        active,
        upstream,
        active_sibling,
        upstream_sibling,
    )


def last_body(chips, quarter):
    def body(roll, strand, grad, mine, received, stream, letters):
        through = mine
        for part in range(chips - 1):
            through = through + received[part].astype(f32)
        grad = grad + through * slope_of_gelu(stream)
        stem = jnp.dot(grad.T.astype(bf16), letters, preferred_element_type=f32)
        parts = [stem[:quarter], stem[quarter:]]
        return choose(strand[0, 0], parts), choose(1 - strand[0, 0], parts).astype(bf16)

    return body


class BlockSum:
    def __init__(self, kept, sends, slot, stages):
        self.kept, self.slot, self.stages = kept, slot, stages
        self.received = self.sent(sends)
        self.done = False

    def sent(self, sends):
        return [seq_swap(part, away) for part, away in zip(sends, distances(self.stages[0])[1:])]

    def last(self):
        return len(self.stages) == 1

    def due(self):
        step = 3 - min(3, len(self.stages))
        return None if self.done else DUE[self.slot][step]

    def join(self):
        self.stages = self.stages[1:]
        parts = len(distances(self.stages[0]))
        rows, width = self.kept.shape
        rows //= parts

        def body(roll, kept, *received):
            total = kept
            for part in received:
                total = total + part.astype(f32)
            return parted(total, parts)

        outs = [((rows, width), f32)] + [((rows, width), bf16)] * (parts - 1)
        self.kept, *sends = run(body, outs, self.kept, *self.received)
        self.received = self.sent(sends)


def distances(bits):
    return [sum(bit for place, bit in enumerate(bits) if (i >> place) & 1) for i in range(1 << len(bits))]


def parted(total, parts):
    rows = total.shape[0] // parts
    pieces_of = [total[i * rows : (i + 1) * rows] for i in range(parts)]
    return [pieces_of[0]] + [piece.astype(bf16) for piece in pieces_of[1:]]


def settle(sums, value, point):
    due = [s for s in sums if s.due() == point]
    value, received = tied(value, [s.received for s in due])
    for s, got in zip(due, received):
        s.received = got
        if s.last():
            s.done = True
        else:
            s.join()
    return value


def assemble(sums, quarter):
    count = len(sums)
    each = 1 + len(sums[0].received)
    half, width = sums[0].kept.shape
    shape = (3, quarter, 2 * half)

    def kernel(*refs):
        out = refs[-1]
        for layer in range(count):
            total = refs[each * layer][...]
            for part in range(1, each):
                total = total + refs[each * layer + part][...].astype(f32)
            total = jnp.concatenate([total[:, : width // 2], total[:, width // 2 :]])
            out[layer] = total.T.reshape(shape)

    return pl.pallas_call(
        kernel,
        out_shape=jax.ShapeDtypeStruct((count,) + shape, f32),
        compiler_params=pltpu.CompilerParams(vmem_limit_bytes=VMEM),
        cost_estimate=pl.CostEstimate(flops=1, bytes_accessed=1, transcendentals=0),
    )(*[value for s in sums for value in [s.kept, *s.received]])


def shards(
    genome, stem_weight, dilated_filter_weight, head_weight, window_start, window_track, targets
):
    shard_rows, pool = genome.shape
    seqs = lax.axis_size("seq")
    chips = lax.axis_size("ch") // CORES
    seq = lax.axis_index("seq")
    strand = lax.axis_index("ch") % CORES
    chip = lax.axis_index("ch") // CORES
    spans = dilations(shard_rows)
    classes = spans[0]
    own_classes = classes // seqs
    steps = shard_rows // classes
    reach = tuple(span // classes * own_classes for span in spans)
    quarter = stem_weight.shape[0]
    channels = dilated_filter_weight.shape[3]
    block = channels // seqs
    tracks = head_weight.shape[1]

    chip_word = jnp.reshape(chip, (1, 1))
    strand_word = jnp.reshape(strand, (1, 1))

    stem_own = [stem_weight] + [chip_shift(stem_weight, by) for by in range(1, chips)]
    quarters = [part for own in stem_own for part in (own, core_swap(own))]

    (blocks,) = run(
        genome_body(steps, seqs, own_classes), [((shard_rows, pool), bf16)], genome
    )
    blocks = lax.all_to_all(
        blocks.reshape(seqs, steps * own_classes, pool), "seq", 0, 0, tiled=True
    )

    sibling_filter = core_swap(dilated_filter_weight)

    own_filter = dilated_filter_weight

    def filter_of(layer):
        return join_filters(strand_word, own_filter, sibling_filter, layer)

    letters, active, stream = stem(
        strand_word, chip_word, blocks.reshape(shard_rows, pool), quarters, chips, own_classes
    )
    row = jnp.arange(shard_rows, dtype=jnp.int32)
    step_of = row // own_classes
    step_of = jnp.where(strand == 0, step_of, shard_rows // own_classes - 1 - step_of)
    class_of = row % own_classes
    position = step_of * classes + seq * own_classes + class_of

    member = (
        (position[:, None] >= window_start[None, :])
        & (position[:, None] < window_start[None, :] + WIN)
    ).astype(bf16)
    counts = jnp.sum((window_track[:, None] == window_track[None, :]).astype(f32), axis=1)
    at_track = (
        jnp.arange(tracks, dtype=jnp.int32)[None, :] == window_track[:, None]
    ).astype(bf16)

    low_first = [(1 << b,) for b in range(seqs.bit_length() - 1)]
    orders = [low_first, low_first[1:] + low_first[:1]]
    place = jnp.arange(channels, dtype=jnp.int32)
    later, local = place // (channels // 2), place % (channels // 2)
    by_distance = []
    for order in orders:
        aways = [0]
        for stage in order:
            aways = [away + far for away in aways for far in distances(stage)]
        away = choose(local // (block // 2), [jnp.full_like(place, away) for away in aways])
        wanted = (seq ^ away) * block + later * (block // 2) + local % (block // 2)
        by_distance.append(
            (wanted[:, None] == jnp.arange(channels, dtype=jnp.int32)[None, :]).astype(bf16)
        )

    filters = [filter_of(0)]
    streams = []
    actives = []
    sibling_actives = []
    for layer in range(LAYERS):
        streams.append(stream)
        for tap in range(3):
            stream = stream + lax.dot_general(
                rolled(active, (tap - 1) * reach[layer]),
                filters[layer][tap],
                (((1,), (1,)), ((), ())),
                preferred_element_type=f32,
            )
        if layer < LAYERS - 1:
            own = jax.nn.gelu(stream).astype(bf16)
            own, own_filter, sibling_filter, by_distance, at_track = tied(
                own, own_filter, sibling_filter, by_distance, at_track
            )
            parts = [chip_shift(own, by) for by in range(1, chips)]
            beside = [
                filter_of(layer + 1),
                placed(by_distance[HIGH_FIRST[LAYERS - 1 - layer]], active),
            ]
            if layer == 1:
                columns = lax.dot_general(
                    head_weight, at_track, (((1,), (1,)), ((), ())), preferred_element_type=f32
                ).astype(bf16)
                beside.append(columns)
            if layer == 2:
                beside.append(jnp.concatenate(by_strand(strand, columns, core_swap(columns))))
            if layer > 0:
                beside.append(core_swap(actives[-1]))
            parts, beside = tied(parts, beside)
            filters.append(beside[0])
            actives.append(beside[1])
            if layer > 0:
                sibling_actives.append(beside[-1])
            if layer == 1:
                columns = beside[2]
            if layer == 2:
                half_columns = beside[2]
            parts = [own] + list(parts)
            active = jnp.concatenate(
                [choose((chip - p) % chips, parts) for p in range(chips)], axis=1
            )

    windows = window_start.shape[0]
    everyone = seqs * chips * CORES
    partial_score, pooled_own, pooled_sent = run(
        score_body(quarter, everyone),
        [((everyone, windows), f32), ((quarter, windows), f32), ((quarter, windows), f32)],
        strand_word,
        stream,
        member,
        half_columns,
    )
    scores = lax.all_to_all(partial_score[:, None], ("seq", "ch"), 0, 0, tiled=True)
    pooled_own = pooled_own + core_swap(pooled_sent)
    pooled_bit = 1
    if pooled_bit < seqs:
        pooled_own = pooled_own + seq_swap(pooled_own.astype(bf16), pooled_bit).astype(f32)
        pooled_bit *= 2
    last_active = placed(by_distance[HIGH_FIRST[0]], active)
    sibling_active = core_swap(actives[-1])
    scores, pooled_own, last_active, sibling_active = tied(
        scores, pooled_own, last_active, sibling_active
    )
    actives.append(last_active)
    sibling_actives.append(sibling_active)
    sibling_actives.append(core_swap(last_active))

    sums = []

    def pooled_step(pooled, value, point):
        total, received, bit, due = pooled
        if not due or due[0] != point:
            return value, pooled
        value, received = tied(value, received)
        total = total + received.astype(f32)
        bit *= 2
        return value, (total, seq_swap(total.astype(bf16), bit) if bit < seqs else None, bit, due[1:])

    pooled = (
        pooled_own,
        seq_swap(pooled_own.astype(bf16), pooled_bit) if pooled_bit < seqs else None,
        pooled_bit,
        POOLED_DUE,
    )
    aligned = (channels // chips) % 128 == 0
    shape = (shard_rows, channels // chips)
    back_outs = [
        (shape, f32),
        (shape, bf16),
        (shape, f32),
        ((chips - 1,) + shape, bf16),
        ((shard_rows, quarter), bf16),
    ]
    state = ()
    for layer in reversed(range(LAYERS)):
        first = layer == LAYERS - 1
        if first:
            window_score, loss_slope, grad, upstream, mine, sends, theirs = run(
                loss_body(reach[layer], chips, quarter),
                [((1, windows), f32)] * 2 + back_outs,
                chip_word,
                strand_word,
                scores[:, 0],
                targets[None],
                counts[None],
                member,
                half_columns,
                filters[layer],
                inside=aligned,
            )
        else:
            grad, upstream, mine, sends, theirs = run(
                back_body(reach[layer], chips, quarter, False),
                back_outs,
                chip_word,
                strand_word,
                *state,
                filters[layer],
                inside=aligned,
            )
        received = jnp.stack([chip_shift(sends[by - 1], by) for by in range(1, chips)])
        slot = LAYERS - 1 - layer
        upstream = settle(sums, upstream, f"middle{slot}")
        kept, *parts = filter_product(
            strand_word,
            actives[layer],
            upstream,
            sibling_actives[layer],
            core_swap(theirs),
            reach[layer],
            quarter,
            2,
        )
        received, kept = tied(received, kept)
        received = settle(sums, received, f"end{slot}")
        received, pooled = pooled_step(pooled, received, f"end{slot}")
        sums.append(BlockSum(kept, parts, slot, orders[HIGH_FIRST[slot]]))
        state = (grad, mine, received, streams[layer])

    stem_shape = (quarter, letters.shape[1])
    stem_keep, stem_away = run(
        last_body(chips, quarter),
        [(stem_shape, f32), (stem_shape, bf16)],
        strand_word,
        *state,
        letters,
        inside=aligned,
    )
    stem_own = stem_keep + core_swap(stem_away).astype(f32)
    stem_send = stem_own.astype(bf16).reshape(seqs, quarter // seqs, -1)
    stem_send = settle(sums, stem_send, "sent")
    stem_send, pooled = pooled_step(pooled, stem_send, "sent")
    stem_blocks = lax.all_to_all(stem_send, "seq", 0, 0, tiled=True)
    stem_blocks = settle(sums, stem_blocks, "summed")
    stem_blocks, pooled = pooled_step(pooled, stem_blocks, "summed")
    stem_block = jnp.sum(stem_blocks.astype(f32), axis=0).astype(bf16)
    stem_grad = lax.all_to_all(
        jnp.broadcast_to(stem_block, (seqs,) + stem_block.shape), "seq", 0, 0, tiled=True
    )
    stem_grad = stem_grad.reshape(quarter, -1).astype(f32)
    pooled_own, received, bit, _ = pooled
    while received is not None:
        pooled_own = pooled_own + received.astype(f32)
        bit *= 2
        received = seq_swap(pooled_own.astype(bf16), bit) if bit < seqs else None
    head_grad = lax.dot_general(
        jnp.concatenate(pieces(0.5 * loss_slope * pooled_own), axis=1),
        jnp.concatenate([at_track] * 3),
        (((1,), (0,)), ((), ())),
        preferred_element_type=f32,
    )
    while any(not s.last() for s in sums):
        for s in sums:
            if not s.last():
                s.join()
    conv_grad = assemble(sums[::-1], quarter)
    return (window_score[0], conv_grad, stem_grad, head_grad)


def solution(mesh):
    return jax.shard_map(
        shards,
        mesh=mesh,
        in_specs=(
            P("seq", None),
            P("ch", None),
            P(None, None, "ch", None),
            P("ch", None),
            P(),
            P(),
            P(),
        ),
        out_specs=(P(), P(None, None, "ch", "seq"), P("ch", None), P("ch", None)),
        check_vma=False,
    )
```

```python
import jax
import jax.numpy as jnp
from jax import lax
from jax.experimental import pallas as pl
from jax.experimental.pallas import tpu as pltpu
from jax.sharding import PartitionSpec as P

LAYERS = 5
WIN = 16
CORES = 2
VMEM = 12 << 20
DUE = (("middle2", "middle3", "end4"), ("middle3", "middle4", "summed"), ("middle4", "end4", "summed"), ("end4", "summed", "needed"), ("end4", "sent", "needed"))
POOLED_DUE = ("sent", "summed")
HIGH_FIRST = (1, 0, 0, 0, 0)

bf16 = jnp.bfloat16
f32 = jnp.float32


def dilations(shard_rows):
    return (shard_rows // 8, shard_rows // 2, shard_rows, 2 * shard_rows, 4 * shard_rows)


def core_swap(value):
    count = lax.axis_size("ch")
    return lax.ppermute(value, "ch", [(i, i ^ 1) for i in range(count)])


def chip_shift(value, by):
    count = lax.axis_size("ch")
    return lax.ppermute(value, "ch", [(i, (i + CORES * by) % count) for i in range(count)])


def seq_swap(value, bit):
    count = lax.axis_size("seq")
    return lax.ppermute(value, "seq", [(i, i ^ bit) for i in range(count)])


def choose(index, options):
    picked = options[0]
    for place, option in enumerate(options[1:], 1):
        picked = jnp.where(index == place, option, picked)
    return picked


def rolled(field, by):
    if by == 0:
        return field
    blank = jnp.zeros((abs(by),) + field.shape[1:], field.dtype)
    if by > 0:
        return jnp.concatenate([field[by:], blank], axis=0)
    return jnp.concatenate([blank, field[:by]], axis=0)


def tied(*values):
    return lax.optimization_barrier(values)


def by_strand(strand, own, sibling):
    return [jnp.where(strand == 0, own, sibling), jnp.where(strand == 0, sibling, own)]


def pieces(value):
    high = value.astype(bf16)
    rest = value - high.astype(f32)
    middle = rest.astype(bf16)
    return high, middle, (rest - middle.astype(f32)).astype(bf16)


def run(body, outs, *values, inside=True):
    if not inside:
        return body(jnp.roll, *values)

    def kernel(*refs):
        results = body(pltpu.roll, *[ref[...] for ref in refs[: len(values)]])
        for ref, result in zip(refs[len(values) :], results):
            ref[...] = result

    return pl.pallas_call(
        kernel,
        out_shape=[jax.ShapeDtypeStruct(shape, kind) for shape, kind in outs],
        compiler_params=pltpu.CompilerParams(vmem_limit_bytes=VMEM),
        cost_estimate=pl.CostEstimate(flops=1, bytes_accessed=1, transcendentals=0),
    )(*values)


def moved(roll, field, by):
    if by == 0:
        return field
    rows = field.shape[0]
    row = lax.broadcasted_iota(jnp.int32, field.shape, 0)
    there = (row + by >= 0) & (row + by < rows)
    return jnp.where(there, roll(field, (-by) % rows, 0), 0.0)


def slope_of_gelu(value):
    scale = 0.7978845608028654
    bend = jnp.tanh(scale * (value + 0.044715 * value * value * value))
    return 0.5 * (1.0 + bend) + 0.5 * value * (1.0 - bend * bend) * scale * (
        1.0 + 3 * 0.044715 * value * value
    )


def back_body(reach, chips, quarter, first):
    def body(roll, chip, strand, grad, *rest):
        if first:
            (taps,) = rest
        else:
            mine, received, stream, taps = rest
            through = mine
            for part in range(chips - 1):
                through = through + received[part].astype(f32)
            grad = grad + through * slope_of_gelu(stream)
        upstream = grad.astype(bf16)
        wide = upstream.astype(f32)
        fields = [moved(roll, wide, (1 - tap) * reach).astype(bf16) for tap in range(3)]
        back = jnp.dot(
            jnp.concatenate(fields, axis=1),
            taps.reshape(-1, taps.shape[-1]),
            preferred_element_type=f32,
        )
        width = grad.shape[1]
        parts = [back[:, i * width : (i + 1) * width] for i in range(chips)]
        index = chip[0, 0]
        sends = [
            choose((index + by) % chips, parts).astype(bf16)[None] for by in range(1, chips)
        ]
        sends = sends[0] if chips == 2 else jnp.concatenate(sends)
        source = lax.broadcasted_iota(jnp.int32, (width, quarter), 0)
        target = lax.broadcasted_iota(jnp.int32, (width, quarter), 1)
        theirs = (source == target + (1 - strand[0, 0]) * quarter).astype(f32).astype(bf16)
        theirs = jnp.dot(upstream, theirs, preferred_element_type=f32).astype(bf16)
        return grad, upstream, choose(index, parts), sends, theirs

    return body


def score_body(quarter, everyone):
    def body(roll, strand, stream, member, columns):
        pooled = sum(
            jnp.dot(term, member, preferred_element_type=f32) for term in pieces(stream.T)
        ) / WIN
        partial = 0.5 * jnp.sum(pooled * columns.astype(f32), axis=0, keepdims=True)
        parts = [pooled[:quarter], pooled[quarter:]]
        return (
            jnp.broadcast_to(partial, (everyone, partial.shape[1])),
            choose(strand[0, 0], parts),
            choose(1 - strand[0, 0], parts),
        )

    return body


def loss_body(reach, chips, quarter):
    back = back_body(reach, chips, quarter, True)

    def body(roll, chip, strand, scores, facts, packed, taps):
        targets, counts = facts[:1], facts[1:]
        rows = packed.shape[0] - CORES * quarter
        member, columns = packed[:rows], packed[rows:]
        score = jnp.sum(scores, axis=0, keepdims=True)
        slope = (jnp.exp(score) - targets) / counts
        grad = sum(
            lax.dot_general(
                term, columns, (((1,), (1,)), ((), ())), preferred_element_type=f32
            )
            for term in pieces(0.5 / WIN * slope * member.astype(f32))
        )
        return (score, slope, *back(roll, chip, strand, grad, taps))

    return body


def genome_body(steps, seqs, own_classes):
    def body(roll, genome):
        rows = genome.shape[0]
        target = lax.broadcasted_iota(jnp.int32, (rows, rows), 0)
        source = lax.broadcasted_iota(jnp.int32, (rows, rows), 1)
        owner, local = target // (steps * own_classes), target % (steps * own_classes)
        step, kind = local // own_classes, local % own_classes
        wanted = step * (seqs * own_classes) + owner * own_classes + kind
        order = (source == wanted).astype(f32).astype(bf16)
        bases = genome.astype(f32).astype(bf16)
        return (jnp.dot(order, bases, preferred_element_type=f32).astype(bf16),)

    return body


def stem(strand, chip, bases, quarters, chips, own_classes):
    rows, pool = bases.shape
    quarter = quarters[0].shape[0]
    width = chips * CORES * quarter

    def kernel(strand_ref, chip_ref, bases_ref, *refs):
        letters_ref, active_ref, stream_ref, weight_ref = refs[len(quarters) :]
        strand, chip = strand_ref[0, 0], chip_ref[0, 0]
        for by in range(chips):
            for core in range(CORES):
                at = (chip + chips - by) % chips * CORES + (strand + core) % CORES
                weight_ref[pl.ds(at * quarter, quarter), :] = refs[by * CORES + core][...]
        target = lax.broadcasted_iota(jnp.int32, (rows, rows), 0)
        source = lax.broadcasted_iota(jnp.int32, (rows, rows), 1)
        step = target // own_classes
        step = jnp.where(strand == 0, step, rows // own_classes - 1 - step)
        order = (source == step * own_classes + target % own_classes).astype(f32).astype(bf16)
        position = lax.broadcasted_iota(jnp.int32, (pool, 4 * pool), 0)
        letter = lax.broadcasted_iota(jnp.int32, (pool, 4 * pool), 1)
        place = jnp.where(strand == 0, letter // 4, pool - 1 - letter // 4)
        spread = (position == place).astype(f32).astype(bf16)
        ordered = jnp.dot(order, bases_ref[...], preferred_element_type=f32).astype(bf16)
        wide = jnp.dot(ordered, spread, preferred_element_type=f32)
        letter = lax.broadcasted_iota(jnp.int32, (rows, 4 * pool), 1) % 4
        base = jnp.where(strand == 0, letter, 3 - letter).astype(f32)
        letters = (wide == base).astype(f32).astype(bf16)
        letters_ref[...] = letters
        whole = lax.dot_general(
            letters, weight_ref[...], (((1,), (1,)), ((), ())), preferred_element_type=f32
        )
        active_ref[...] = jax.nn.gelu(whole).astype(bf16)
        each = width // chips
        stream_ref[...] = choose(chip, [whole[:, i * each : (i + 1) * each] for i in range(chips)])

    return pl.pallas_call(
        kernel,
        out_shape=[
            jax.ShapeDtypeStruct((rows, 4 * pool), bf16),
            jax.ShapeDtypeStruct((rows, width), bf16),
            jax.ShapeDtypeStruct((rows, width // chips), f32),
        ],
        in_specs=[pl.BlockSpec(memory_space=pltpu.SMEM)] * 2
        + [pl.BlockSpec(memory_space=pltpu.VMEM)] * (1 + len(quarters)),
        scratch_shapes=[pltpu.VMEM((width, 4 * pool), bf16)],
        compiler_params=pltpu.CompilerParams(vmem_limit_bytes=VMEM),
        cost_estimate=pl.CostEstimate(flops=1, bytes_accessed=1, transcendentals=0),
    )(strand, chip, bases, *quarters)


def join_filters(strand, own, sibling, layer):
    taps, quarter, channels = own.shape[1:]

    def kernel(strand_ref, own_ref, sibling_ref, out_ref, sems):
        copies = [
            pltpu.make_async_copy(
                ref.at[layer], out_ref.at[:, pl.ds(at * quarter, quarter), :], sems.at[core]
            )
            for core, (ref, at) in enumerate(
                [(own_ref, strand_ref[0, 0]), (sibling_ref, 1 - strand_ref[0, 0])]
            )
        ]
        for copy in copies:
            copy.start()
        for copy in copies:
            copy.wait()

    return pl.pallas_call(
        kernel,
        out_shape=jax.ShapeDtypeStruct((taps, CORES * quarter, channels), bf16),
        in_specs=[
            pl.BlockSpec(memory_space=pltpu.SMEM),
            pl.BlockSpec(memory_space=pltpu.HBM),
            pl.BlockSpec(memory_space=pltpu.HBM),
        ],
        out_specs=pl.BlockSpec(memory_space=pl.ANY),
        scratch_shapes=[pltpu.SemaphoreType.DMA((CORES,))],
        compiler_params=pltpu.CompilerParams(vmem_limit_bytes=VMEM),
        cost_estimate=pl.CostEstimate(flops=1, bytes_accessed=1, transcendentals=0),
    )(strand, own, sibling)


def placed(order, active):
    def body(roll, order, active):
        return (
            lax.dot_general(
                order, active, (((1,), (1,)), ((), ())), preferred_element_type=f32
            ).astype(bf16),
        )

    return run(body, [((order.shape[0], active.shape[0]), bf16)], order, active)[0]


def tap_rows(roll, upstream, offset, reach, quarter):
    width = 3 * quarter
    shape = (upstream.shape[1], 2 * width)
    source = lax.broadcasted_iota(jnp.int32, shape, 0)
    target = lax.broadcasted_iota(jnp.int32, shape, 1)
    target = jnp.where(target >= width, target - width, target)
    tap = (target >= quarter).astype(jnp.int32) + (target >= 2 * quarter).astype(jnp.int32)
    spread = (source == offset + target - tap * quarter).astype(f32).astype(bf16)
    wide = jnp.dot(upstream, spread, preferred_element_type=f32)
    lane = lax.broadcasted_iota(jnp.int32, wide.shape, 1)
    late = lane >= width
    lane = jnp.where(late, lane - width, lane)
    low, high = moved(roll, wide, reach), moved(roll, wide, -reach)
    taps = jnp.where(lane < quarter, low, jnp.where(lane < 2 * quarter, wide, high))
    return [jnp.where(late, 0.0, taps).astype(bf16), jnp.where(late, taps, 0.0).astype(bf16)]


def filter_product(strand, active, upstream, active_sibling, upstream_sibling, reach, quarter, parts):
    half = active.shape[0] // 2

    def body(roll, strand, active, upstream, active_sibling, upstream_sibling):
        fields = [active[:half], active[half:], active_sibling[:half], active_sibling[half:]]
        taps = tap_rows(roll, upstream, strand[0, 0] * quarter, reach, quarter)
        taps = taps + tap_rows(roll, upstream_sibling, 0, reach, quarter)
        total = jnp.dot(
            jnp.concatenate(fields, axis=1), jnp.concatenate(taps), preferred_element_type=f32
        )
        return parted(total, parts)

    shape = (half // parts, 6 * quarter)
    return run(
        body,
        [(shape, f32)] + [(shape, bf16)] * (parts - 1),
        strand,
        active,
        upstream,
        active_sibling,
        upstream_sibling,
    )


def last_body(chips, quarter):
    def body(roll, strand, grad, mine, received, stream, letters):
        through = mine
        for part in range(chips - 1):
            through = through + received[part].astype(f32)
        grad = grad + through * slope_of_gelu(stream)
        stem = jnp.dot(grad.T.astype(bf16), letters, preferred_element_type=f32)
        parts = [stem[:quarter], stem[quarter:]]
        return choose(strand[0, 0], parts), choose(1 - strand[0, 0], parts).astype(bf16)

    return body


class BlockSum:
    def __init__(self, kept, sends, slot, stages):
        self.kept, self.slot, self.stages = kept, slot, stages
        self.received = self.sent(sends)
        self.done = False

    def sent(self, sends):
        return [seq_swap(part, away) for part, away in zip(sends, distances(self.stages[0])[1:])]

    def last(self):
        return len(self.stages) == 1

    def due(self):
        step = 3 - min(3, len(self.stages))
        return None if self.done else DUE[self.slot][step]

    def join(self):
        self.stages = self.stages[1:]
        parts = len(distances(self.stages[0]))
        rows, width = self.kept.shape
        rows //= parts

        def body(roll, kept, *received):
            total = kept
            for part in received:
                total = total + part.astype(f32)
            return parted(total, parts)

        outs = [((rows, width), f32)] + [((rows, width), bf16)] * (parts - 1)
        self.kept, *sends = run(body, outs, self.kept, *self.received)
        self.received = self.sent(sends)


def distances(bits):
    return [sum(bit for place, bit in enumerate(bits) if (i >> place) & 1) for i in range(1 << len(bits))]


def parted(total, parts):
    rows = total.shape[0] // parts
    pieces_of = [total[i * rows : (i + 1) * rows] for i in range(parts)]
    return [pieces_of[0]] + [piece.astype(bf16) for piece in pieces_of[1:]]


def settle(sums, value, point):
    due = [s for s in sums if s.due() == point]
    value, received = tied(value, [s.received for s in due])
    for s, got in zip(due, received):
        s.received = got
        if s.last():
            s.done = True
        else:
            s.join()
    return value


def assemble(sums, quarter):
    count = len(sums)
    each = 1 + len(sums[0].received)
    half, width = sums[0].kept.shape
    shape = (3, quarter, 2 * half)

    def kernel(*refs):
        out = refs[-1]
        for layer in range(count):
            total = refs[each * layer][...]
            for part in range(1, each):
                total = total + refs[each * layer + part][...].astype(f32)
            total = jnp.concatenate([total[:, : width // 2], total[:, width // 2 :]])
            out[layer] = total.T.reshape(shape)

    return pl.pallas_call(
        kernel,
        out_shape=jax.ShapeDtypeStruct((count,) + shape, f32),
        compiler_params=pltpu.CompilerParams(vmem_limit_bytes=VMEM),
        cost_estimate=pl.CostEstimate(flops=1, bytes_accessed=1, transcendentals=0),
    )(*[value for s in sums for value in [s.kept, *s.received]])


def shards(
    genome, stem_weight, dilated_filter_weight, head_weight, window_start, window_track, targets
):
    shard_rows, pool = genome.shape
    seqs = lax.axis_size("seq")
    chips = lax.axis_size("ch") // CORES
    seq = lax.axis_index("seq")
    strand = lax.axis_index("ch") % CORES
    chip = lax.axis_index("ch") // CORES
    spans = dilations(shard_rows)
    classes = spans[0]
    own_classes = classes // seqs
    steps = shard_rows // classes
    reach = tuple(span // classes * own_classes for span in spans)
    quarter = stem_weight.shape[0]
    channels = dilated_filter_weight.shape[3]
    block = channels // seqs
    tracks = head_weight.shape[1]

    chip_word = jnp.reshape(chip, (1, 1))
    strand_word = jnp.reshape(strand, (1, 1))

    stem_own = [stem_weight] + [chip_shift(stem_weight, by) for by in range(1, chips)]
    quarters = [part for own in stem_own for part in (own, core_swap(own))]

    (blocks,) = run(
        genome_body(steps, seqs, own_classes), [((shard_rows, pool), bf16)], genome
    )
    blocks = lax.all_to_all(
        blocks.reshape(seqs, steps * own_classes, pool), "seq", 0, 0, tiled=True
    )

    sibling_filter = core_swap(dilated_filter_weight)

    own_filter = dilated_filter_weight

    def filter_of(layer):
        return join_filters(strand_word, own_filter, sibling_filter, layer)

    letters, active, stream = stem(
        strand_word, chip_word, blocks.reshape(shard_rows, pool), quarters, chips, own_classes
    )
    row = jnp.arange(shard_rows, dtype=jnp.int32)
    step_of = row // own_classes
    step_of = jnp.where(strand == 0, step_of, shard_rows // own_classes - 1 - step_of)
    class_of = row % own_classes
    position = step_of * classes + seq * own_classes + class_of

    member = (
        (position[:, None] >= window_start[None, :])
        & (position[:, None] < window_start[None, :] + WIN)
    ).astype(bf16)
    counts = jnp.sum((window_track[:, None] == window_track[None, :]).astype(f32), axis=1)
    at_track = (
        jnp.arange(tracks, dtype=jnp.int32)[None, :] == window_track[:, None]
    ).astype(bf16)

    low_first = [(1 << b,) for b in range(seqs.bit_length() - 1)]
    orders = [low_first, low_first[1:] + low_first[:1]]
    place = jnp.arange(channels, dtype=jnp.int32)
    later, local = place // (channels // 2), place % (channels // 2)
    by_distance = []
    for order in orders:
        aways = [0]
        for stage in order:
            aways = [away + far for away in aways for far in distances(stage)]
        away = choose(local // (block // 2), [jnp.full_like(place, away) for away in aways])
        wanted = (seq ^ away) * block + later * (block // 2) + local % (block // 2)
        by_distance.append(
            (wanted[:, None] == jnp.arange(channels, dtype=jnp.int32)[None, :]).astype(bf16)
        )

    filters = [filter_of(0)]
    streams = []
    actives = []
    sibling_actives = []
    for layer in range(LAYERS):
        streams.append(stream)
        for tap in range(3):
            stream = stream + lax.dot_general(
                rolled(active, (tap - 1) * reach[layer]),
                filters[layer][tap],
                (((1,), (1,)), ((), ())),
                preferred_element_type=f32,
            )
        if layer < LAYERS - 1:
            own = jax.nn.gelu(stream).astype(bf16)
            own, own_filter, sibling_filter, by_distance, at_track = tied(
                own, own_filter, sibling_filter, by_distance, at_track
            )
            parts = [chip_shift(own, by) for by in range(1, chips)]
            beside = [
                filter_of(layer + 1),
                placed(by_distance[HIGH_FIRST[LAYERS - 1 - layer]], active),
            ]
            if layer == 1:
                columns = lax.dot_general(
                    head_weight, at_track, (((1,), (1,)), ((), ())), preferred_element_type=f32
                ).astype(bf16)
                beside.append(columns)
            if layer == 2:
                beside.append(jnp.concatenate(by_strand(strand, columns, core_swap(columns))))
            if layer > 0:
                beside.append(core_swap(actives[-1]))
            parts, beside = tied(parts, beside)
            filters.append(beside[0])
            actives.append(beside[1])
            if layer > 0:
                sibling_actives.append(beside[-1])
            if layer == 1:
                columns = beside[2]
            if layer == 2:
                half_columns = beside[2]
            parts = [own] + list(parts)
            active = jnp.concatenate(
                [choose((chip - p) % chips, parts) for p in range(chips)], axis=1
            )

    facts = jnp.stack([targets, counts])
    packed = jnp.concatenate([member, half_columns])
    stream, facts, packed = tied(stream, facts, packed)
    windows = window_start.shape[0]
    everyone = seqs * chips * CORES
    partial_score, pooled_own, pooled_sent = run(
        score_body(quarter, everyone),
        [((everyone, windows), f32), ((quarter, windows), f32), ((quarter, windows), f32)],
        strand_word,
        stream,
        member,
        half_columns,
    )
    scores = lax.all_to_all(partial_score[:, None], ("seq", "ch"), 0, 0, tiled=True)
    pooled_own = pooled_own + core_swap(pooled_sent)
    pooled_bit = 1
    if pooled_bit < seqs:
        pooled_own = pooled_own + seq_swap(pooled_own.astype(bf16), pooled_bit).astype(f32)
        pooled_bit *= 2
    last_active = placed(by_distance[HIGH_FIRST[0]], active)
    sibling_active = core_swap(actives[-1])
    scores, pooled_own, last_active, sibling_active = tied(
        scores, pooled_own, last_active, sibling_active
    )
    actives.append(last_active)
    sibling_actives.append(sibling_active)
    sibling_actives.append(core_swap(last_active))

    sums = []

    def pooled_step(pooled, value, point):
        total, received, bit, due = pooled
        if not due or due[0] != point:
            return value, pooled
        value, received = tied(value, received)
        total = total + received.astype(f32)
        bit *= 2
        return value, (total, seq_swap(total.astype(bf16), bit) if bit < seqs else None, bit, due[1:])

    pooled = (
        pooled_own,
        seq_swap(pooled_own.astype(bf16), pooled_bit) if pooled_bit < seqs else None,
        pooled_bit,
        POOLED_DUE,
    )
    aligned = (channels // chips) % 128 == 0
    shape = (shard_rows, channels // chips)
    back_outs = [
        (shape, f32),
        (shape, bf16),
        (shape, f32),
        ((chips - 1,) + shape, bf16),
        ((shard_rows, quarter), bf16),
    ]
    state = ()
    for layer in reversed(range(LAYERS)):
        first = layer == LAYERS - 1
        if first:
            window_score, loss_slope, grad, upstream, mine, sends, theirs = run(
                loss_body(reach[layer], chips, quarter),
                [((1, windows), f32)] * 2 + back_outs,
                chip_word,
                strand_word,
                scores[:, 0],
                facts,
                packed,
                filters[layer],
                inside=aligned,
            )
        else:
            grad, upstream, mine, sends, theirs = run(
                back_body(reach[layer], chips, quarter, False),
                back_outs,
                chip_word,
                strand_word,
                *state,
                filters[layer],
                inside=aligned,
            )
        received = jnp.stack([chip_shift(sends[by - 1], by) for by in range(1, chips)])
        slot = LAYERS - 1 - layer
        upstream = settle(sums, upstream, f"middle{slot}")
        kept, *parts = filter_product(
            strand_word,
            actives[layer],
            upstream,
            sibling_actives[layer],
            core_swap(theirs),
            reach[layer],
            quarter,
            2,
        )
        received, kept = tied(received, kept)
        received = settle(sums, received, f"end{slot}")
        received, pooled = pooled_step(pooled, received, f"end{slot}")
        sums.append(BlockSum(kept, parts, slot, orders[HIGH_FIRST[slot]]))
        state = (grad, mine, received, streams[layer])

    stem_shape = (quarter, letters.shape[1])
    stem_keep, stem_away = run(
        last_body(chips, quarter),
        [(stem_shape, f32), (stem_shape, bf16)],
        strand_word,
        *state,
        letters,
        inside=aligned,
    )
    stem_own = stem_keep + core_swap(stem_away).astype(f32)
    stem_send = stem_own.astype(bf16).reshape(seqs, quarter // seqs, -1)
    stem_send = settle(sums, stem_send, "sent")
    stem_send, pooled = pooled_step(pooled, stem_send, "sent")
    stem_blocks = lax.all_to_all(stem_send, "seq", 0, 0, tiled=True)
    stem_blocks = settle(sums, stem_blocks, "summed")
    stem_blocks, pooled = pooled_step(pooled, stem_blocks, "summed")
    stem_block = jnp.sum(stem_blocks.astype(f32), axis=0).astype(bf16)
    stem_grad = lax.all_to_all(
        jnp.broadcast_to(stem_block, (seqs,) + stem_block.shape), "seq", 0, 0, tiled=True
    )
    stem_grad = stem_grad.reshape(quarter, -1).astype(f32)
    pooled_own, received, bit, _ = pooled
    while received is not None:
        pooled_own = pooled_own + received.astype(f32)
        bit *= 2
        received = seq_swap(pooled_own.astype(bf16), bit) if bit < seqs else None
    head_grad = lax.dot_general(
        jnp.concatenate(pieces(0.5 * loss_slope * pooled_own), axis=1),
        jnp.concatenate([at_track] * 3),
        (((1,), (0,)), ((), ())),
        preferred_element_type=f32,
    )
    while any(not s.last() for s in sums):
        for s in sums:
            if not s.last():
                s.join()
    conv_grad = assemble(sums[::-1], quarter)
    return (window_score[0], conv_grad, stem_grad, head_grad)


def solution(mesh):
    return jax.shard_map(
        shards,
        mesh=mesh,
        in_specs=(
            P("seq", None),
            P("ch", None),
            P(None, None, "ch", None),
            P("ch", None),
            P(),
            P(),
            P(),
        ),
        out_specs=(P(), P(None, None, "ch", "seq"), P("ch", None), P("ch", None)),
        check_vma=False,
    )
```
